128 devices in a mesh: seq: 8 (over y, core), enc: 16 (over z, x).
Axes of the slice: x: 4, y: 4, z: 4, core: 2. Of those that a mesh axis runs over, the one named last changes fastest.
Arguments:
- hidden: bfloat16 [2048, 8192], P('seq', 'enc'), may hold values from -56 to 56
- query_weight: bfloat16 [8192, 8192], P(None, 'enc'), may hold values from -0.0625 to 0.0625
- key_weight: bfloat16 [2048, 8192], P(None, 'enc'), may hold values from -0.125 to 0.125
- value_weight: bfloat16 [2048, 8192], P(None, 'enc'), may hold values from -0.125 to 0.125
- output_weight: bfloat16 [8192, 8192], P('enc'), may hold values from -0.0625 to 0.0625
- neighbour_states: bfloat16 [128, 128, 2048], P('enc', None, 'seq'), may hold values from -6 to 6
- neighbour_slot: int32 [32, 2], P('seq'), may hold values from 0 to 127, as said below
- d_output: bfloat16 [2048, 8192], P('seq', 'enc'), may hold values from -6 to 6
Outputs:
- output: bfloat16 [2048, 8192], P('seq', 'enc')
- d_hidden: bfloat16 [2048, 8192], P('seq', 'enc')
- d_states: bfloat16 [128, 128, 2048], P('enc', None, 'seq')
The draws below stay inside these ranges and needn't reach their ends.
Inputs may be any that keep to these rules, and one draw needn't show every extreme that they name: `neighbour_slot`: each entry is e * 8 + s + b, where e is the encoder shard that holds the neighbour, s the seq index holding the span that reads it, and b below 1; no two entries are equal; in every draw some bucket of 1 slots is full.
All inputs are finite; a program needn't handle non-finite values.
Results may differ from the reference program's by a relative error of at most 0.02.
Values may be sent and summed in bfloat16 or wider, within the bound.
No kernel may reach another device: no remote copies, remote signals or barrier semaphores. Data moves between devices by JAX's collectives and lax.ppermute only.
A program may use at most 128 MiB of HBM per device.

```python
import jax
import jax.numpy as jnp
from jax import lax

D = 8192
HEADS = 64
HEAD = 128
ENC_WIDTH = 2048
NEIGH_LEN = 128
SPAN = 64
NEIGHBOURS = 2
SPANS_DEV = 4
BUCKET = 1
SPANS = 32
TOKENS = 2048
SLOTS = 128
N_SEQ = 8
N_ENC = 16


def draw_hidden(key, part):
    key = jax.random.fold_in(key, 11)
    key_values = jax.random.fold_in(key, 0)
    values = jnp.clip(jax.random.normal(key_values, (TOKENS, D), jnp.float32), -6.0, 6.0)
    return values.astype(jnp.bfloat16)


def draw_neighbour_slot(key, part):
    key = jax.random.fold_in(key, 5)
    group_keys = jax.random.split(key, N_SEQ)
    orders = jax.vmap(lambda single: jax.random.permutation(single, N_ENC))(group_keys)
    per_group = NEIGHBOURS * SPANS_DEV
    order_rank = jnp.arange(per_group, dtype=jnp.int32)
    shard_index = orders[:, order_rank % N_ENC].astype(jnp.int32)
    group_index = jnp.arange(N_SEQ, dtype=jnp.int32)[:, None]
    slot_index = shard_index * (N_SEQ * BUCKET) + group_index * BUCKET + (order_rank // N_ENC)[None, :]
    return slot_index.reshape(SPANS, NEIGHBOURS).astype(jnp.int32)


def block_levels(key, dims, shards, smallest, largest):
    factor_of = 1.0
    for dim, blocks in shards:
        draws = jax.random.uniform(jax.random.fold_in(jax.random.fold_in(key, 6), dim), (blocks,), jnp.float32, smallest / len(shards), largest / len(shards))
        factor_of = factor_of * jnp.repeat(jnp.exp(draws), dims[dim] // blocks).reshape((-1,) + (1,) * (len(dims) - 1 - dim))
    return factor_of


def bell_draw(key, shape, scale, bound, shards=(), held_as=jnp.bfloat16):
    values = scale * jax.random.normal(key, shape, jnp.float32)
    if shards:
        values = values * block_levels(key, shape, shards, -0.22, 0.18)
    return jnp.clip(values, -bound, bound).astype(held_as)


def setup_inputs(seed: int = 0) -> dict:
    splits = jax.random.split(jax.random.key(seed), 9)
    return {
        "hidden": draw_hidden(jax.random.fold_in(splits[8], 71), 0),
        "query_weight": bell_draw(splits[1], (D, HEADS * HEAD), D ** -0.5, 0.0625, ((1, 16),)),
        "key_weight": bell_draw(splits[2], (ENC_WIDTH, HEADS * HEAD), ENC_WIDTH ** -0.5, 0.125, ((1, 16),)),
        "value_weight": bell_draw(splits[3], (ENC_WIDTH, HEADS * HEAD), ENC_WIDTH ** -0.5, 0.125, ((1, 16),)),
        "output_weight": bell_draw(splits[4], (HEADS * HEAD, D), (HEADS * HEAD) ** -0.5, 0.0625, ((0, 16),)),
        "neighbour_states": bell_draw(splits[5], (SLOTS, NEIGH_LEN, ENC_WIDTH), 1.0, 6.0, ((0, 16), (2, 8))),
        "neighbour_slot": draw_neighbour_slot(jax.random.fold_in(splits[8], 71), 0),
        "d_output": bell_draw(splits[7], (TOKENS, D), 1.0, 6.0, ((0, 8), (1, 16))),
    }


def lowered(matrix):
    return lax.optimization_barrier(matrix.astype(jnp.bfloat16)).astype(jnp.float32)


def grouped_sum(left_groups, right_groups):
    def accumulate(running, operands):
        product = jnp.dot(operands[0], operands[1], preferred_element_type=jnp.float32)
        return running + lowered(product), None

    start_value = jnp.zeros((left_groups.shape[1], right_groups.shape[2]), jnp.float32)
    running, _ = lax.scan(accumulate, start_value, (left_groups, right_groups))
    return running


def split_columns(matrix, width):
    return matrix.reshape(matrix.shape[0], N_ENC, width).transpose(1, 0, 2)


def reference(hidden, query_weight, key_weight, value_weight, output_weight, neighbour_states, neighbour_slot, d_output):
    score_scale = HEAD ** -0.5
    group_cols = HEADS * HEAD // N_ENC
    queries = jnp.dot(hidden, query_weight, preferred_element_type=jnp.float32).astype(jnp.bfloat16)
    flat_slot = neighbour_slot.reshape(-1).astype(jnp.int32)
    chosen = jnp.take(neighbour_states, flat_slot, axis=0).reshape(-1, ENC_WIDTH)
    key_rows = jnp.dot(chosen, key_weight, preferred_element_type=jnp.float32).astype(jnp.bfloat16)
    value_rows = jnp.dot(chosen, value_weight, preferred_element_type=jnp.float32).astype(jnp.bfloat16)
    query_four = queries.astype(jnp.float32).reshape(SPANS, SPAN, HEADS, HEAD)
    key_four = key_rows.astype(jnp.float32).reshape(SPANS, NEIGHBOURS * NEIGH_LEN, HEADS, HEAD)
    value_four = value_rows.astype(jnp.float32).reshape(SPANS, NEIGHBOURS * NEIGH_LEN, HEADS, HEAD)
    scores = jnp.einsum("cqhd,ckhd->chqk", query_four, key_four) * score_scale
    exponent = jnp.exp(scores - jnp.max(scores, axis=-1, keepdims=True))
    attention = exponent / jnp.sum(exponent, axis=-1, keepdims=True)
    attention_low = lowered(attention)
    context = jnp.einsum("chqk,ckhd->cqhd", attention_low, value_four).astype(jnp.bfloat16)
    context = context.reshape(TOKENS, HEADS * HEAD)
    output = grouped_sum(split_columns(context, group_cols), output_weight.reshape(N_ENC, group_cols, D))
    output = output.astype(jnp.bfloat16)

    d_context = jnp.dot(d_output, output_weight.T, preferred_element_type=jnp.float32).astype(jnp.bfloat16)
    d_four = d_context.astype(jnp.float32).reshape(SPANS, SPAN, HEADS, HEAD)
    d_attention = jnp.einsum("cqhd,ckhd->chqk", d_four, value_four)
    inner_sum = jnp.sum(attention * d_attention, axis=-1, keepdims=True)
    d_scores = lowered(attention * (d_attention - inner_sum) * score_scale)
    d_queries = jnp.einsum("chqk,ckhd->cqhd", d_scores, key_four).astype(jnp.bfloat16)
    d_queries = d_queries.reshape(TOKENS, HEADS * HEAD)
    d_keys = jnp.einsum("chqk,cqhd->ckhd", d_scores, query_four).astype(jnp.bfloat16)
    d_values = jnp.einsum("chqk,cqhd->ckhd", attention_low, d_four).astype(jnp.bfloat16)
    d_keys = d_keys.reshape(-1, HEADS * HEAD)
    d_values = d_values.reshape(-1, HEADS * HEAD)
    d_hidden = grouped_sum(split_columns(d_queries, group_cols), query_weight.T.reshape(N_ENC, group_cols, D))
    d_hidden = d_hidden.astype(jnp.bfloat16)
    left_groups = jnp.concatenate([split_columns(d_keys, group_cols), split_columns(d_values, group_cols)], axis=2)
    right_groups = jnp.concatenate([key_weight.T.reshape(N_ENC, group_cols, ENC_WIDTH), value_weight.T.reshape(N_ENC, group_cols, ENC_WIDTH)], axis=1)
    slot_grads = grouped_sum(left_groups, right_groups).reshape(SPANS * NEIGHBOURS, NEIGH_LEN, ENC_WIDTH)
    d_states = jnp.zeros((SLOTS, NEIGH_LEN, ENC_WIDTH), jnp.float32).at[flat_slot].set(slot_grads)
    return output, d_hidden, d_states.astype(jnp.bfloat16)
```

```python
import functools

import jax
import jax.numpy as jnp
from jax import lax
from jax.experimental import pallas as pl
from jax.experimental.pallas import tpu as pltpu
from jax.sharding import PartitionSpec as P

HEAD = 128
SPAN = 64
SEQ = 8
SIDE = 4
ENC = SIDE * SIDE
BF = jnp.bfloat16
F32 = jnp.float32
AXES = ("seq", "enc")
NT = (((1,), (1,)), ((), ()))
NN = (((1,), (0,)), ((), ()))
TN = (((0,), (0,)), ((), ()))


def dot(a, b, dims):
    return lax.dot_general(a, b, dims, preferred_element_type=F32)


def shift_table(long_phase, shift):
    pairs = []
    for seq in range(SEQ):
        for z in range(SIDE):
            for x in range(SIDE):
                if (seq % 2 == 0) == long_phase:
                    to_z, to_x = (z + shift) % SIDE, x
                else:
                    to_z, to_x = z, (x + shift) % SIDE
                pairs.append((seq * ENC + z * SIDE + x, seq * ENC + to_z * SIDE + to_x))
    return pairs


def move_u(value, shift):
    return lax.ppermute(value, AXES, shift_table(False, shift))


def move_v(value, shift):
    return lax.ppermute(value, AXES, shift_table(True, shift))


def relative_index():
    seq, enc = lax.axis_index("seq"), lax.axis_index("enc")
    z, x = enc // SIDE, enc % SIDE
    even = seq % 2 == 0
    u, v = jnp.where(even, x, z), jnp.where(even, z, x)
    k = lax.broadcasted_iota(jnp.int32, (SIDE, SIDE), 0)
    j = lax.broadcasted_iota(jnp.int32, (SIDE, SIDE), 1)
    uu, vv = (u - j) % SIDE, (v - k) % SIDE
    return jnp.where(even, vv * SIDE + uu, uu * SIDE + vv).astype(jnp.int32)


def gather_short(own):
    one, two, three = move_u(own, 1), move_u(own, 2), move_u(own, -1)
    return jnp.stack([own, one, two, three])


def gather_long(group):
    one, three = move_v(group, 1), move_v(group, -1)
    return one, three


def gather_last(one, three):
    return move_v(one[:2], 1), move_v(three[2:], -1)


def params():
    return pltpu.CompilerParams(vmem_limit_bytes=24 * 1024 * 1024)


def accumulate_kernel(count, has_start, dims, index_ref, *refs):
    x_refs, w_refs = refs[:count], refs[count : 2 * count]
    start_ref = refs[2 * count] if has_start else None
    out_ref, total = refs[-2], refs[-1]
    step = pl.program_id(0)

    @pl.when(step == 0)
    def _():
        total[...] = start_ref[...] if has_start else jnp.zeros_like(total)

    for x_ref, w_ref in zip(x_refs, w_refs):
        total[...] += dot(x_ref[0], w_ref[...], dims)

    @pl.when(step == pl.num_programs(0) - 1)
    def _():
        out_ref[...] = total[...].astype(out_ref.dtype)


def gathered_dot(index, buffers, weight, by_rows, start, out_type):
    count, steps = len(buffers), buffers[0].shape[0]
    rows, width = buffers[0].shape[1:]
    dims = NN if by_rows else NT

    def weight_spec(b):
        if by_rows:
            return pl.BlockSpec((width, weight.shape[1]), lambda i, ix: (ix[b * steps + i], 0))
        return pl.BlockSpec((weight.shape[0], width), lambda i, ix: (0, ix[b * steps + i]))

    cols = weight.shape[1] if by_rows else weight.shape[0]
    in_specs = [pl.BlockSpec((1, rows, width), lambda i, ix: (i, 0, 0))] * count
    in_specs += [weight_spec(b) for b in range(count)]
    operands = list(buffers) + [weight] * count
    if start is not None:
        in_specs.append(pl.BlockSpec((rows, cols), lambda i, ix: (0, 0)))
        operands.append(start)
    return pl.pallas_call(
        functools.partial(accumulate_kernel, count, start is not None, dims),
        out_shape=jax.ShapeDtypeStruct((rows, cols), out_type),
        grid_spec=pltpu.PrefetchScalarGridSpec(
            num_scalar_prefetch=1,
            grid=(steps,),
            in_specs=in_specs,
            out_specs=pl.BlockSpec((rows, cols), lambda i, ix: (0, 0)),
            scratch_shapes=[pltpu.VMEM((rows, cols), F32)],
        ),
        compiler_params=params(),
        cost_estimate=pl.CostEstimate(
            flops=2 * count * steps * rows * width * cols,
            bytes_accessed=2 * count * steps * (rows + cols) * width,
            transcendentals=0,
        ),
    )(index.reshape(-1), *operands)


def far_kernel(dims, index_ref, x_ref, wa_ref, wb_ref, a_ref, b_ref):
    a_ref[0] = dot(x_ref[...], wa_ref[...], dims).astype(BF)
    b_ref[0] = dot(x_ref[...], wb_ref[...], dims).astype(BF)


def side_kernel(dims, index_ref, x_ref, w3_ref, w1_ref, a_ref, b_ref, g3_ref, g1_ref):
    first = pl.program_id(0) < 2
    g3 = dot(x_ref[...], w3_ref[...], dims)
    g1 = dot(x_ref[...], w1_ref[...], dims)
    a, b = a_ref[0].astype(F32), b_ref[0].astype(F32)
    g3_ref[0] = (g3 + jnp.where(first, a, 0.0)).astype(BF)
    g1_ref[0] = (g1 + jnp.where(first, 0.0, b)).astype(BF)


def near_kernel(dims, index_ref, x_ref, w_ref, r3_ref, r1_ref, *t_refs):
    step = pl.program_id(0)
    value = dot(x_ref[...], w_ref[...], dims) + r3_ref[0].astype(F32) + r1_ref[0].astype(F32)
    for j, t_ref in enumerate(t_refs):

        @pl.when(step == j)
        def _():
            t_ref[...] = value.astype(BF)


def scatter_sum(index, x, weight, by_rows):
    rows, inner = x.shape
    width = weight.shape[0] // ENC if by_rows else weight.shape[1] // ENC
    dims = NT if by_rows else NN

    def weight_spec(pick):
        if by_rows:
            return pl.BlockSpec((width, inner), lambda i, ix: (ix[pick(i)], 0))
        return pl.BlockSpec((inner, width), lambda i, ix: (0, ix[pick(i)]))

    x_spec = pl.BlockSpec((rows, inner), lambda i, ix: (0, 0))
    block = pl.BlockSpec((1, rows, width), lambda i, ix: (i, 0, 0))
    half = jax.ShapeDtypeStruct((2, rows, width), BF)
    whole = jax.ShapeDtypeStruct((4, rows, width), BF)
    one = jax.ShapeDtypeStruct((rows, width), BF)
    flat = index.reshape(-1)

    def call(kernel, steps, picks, extra_specs, extra, out_shape, out_specs):
        terms = steps * len(picks)
        return pl.pallas_call(
            functools.partial(kernel, dims),
            out_shape=out_shape,
            grid_spec=pltpu.PrefetchScalarGridSpec(
                num_scalar_prefetch=1,
                grid=(steps,),
                in_specs=[x_spec] + [weight_spec(pick) for pick in picks] + extra_specs,
                out_specs=out_specs,
            ),
            compiler_params=params(),
            cost_estimate=pl.CostEstimate(
                flops=2 * terms * rows * inner * width,
                bytes_accessed=2 * terms * (inner + 2 * rows) * width,
                transcendentals=0,
            ),
        )(flat, x, *([weight] * len(picks)), *extra)

    far_a, far_b = call(
        far_kernel, 2, [lambda i: 8 + i, lambda i: 10 + i], [], [], [half, half], [block, block]
    )
    from_a, from_b = move_v(far_a, 1), move_v(far_b, -1)
    low = pl.BlockSpec((1, rows, width), lambda i, ix: (jnp.minimum(i, 1), 0, 0))
    high = pl.BlockSpec((1, rows, width), lambda i, ix: (jnp.maximum(i - 2, 0), 0, 0))
    g3, g1 = call(
        side_kernel, 4, [lambda i: 12 + i, lambda i: 4 + i], [low, high], [from_a, from_b],
        [whole, whole], [block, block],
    )
    r3, r1 = move_v(g3, 1), move_v(g1, -1)
    pieces = call(
        near_kernel, 4, [lambda i: i], [block, block], [r3, r1], [one] * 4,
        [pl.BlockSpec((rows, width), lambda i, ix: (0, 0))] * 4,
    )
    return scatter_short(pieces)


def scatter_short(pieces):
    t0, t1, t2, t3 = pieces
    q1, q2, q3 = move_u(t1, -1), move_u(t2, 2), move_u(t3, 1)
    total = t0.astype(F32) + q1.astype(F32) + q2.astype(F32) + q3.astype(F32)
    return total.astype(BF)


def pair_kernel(extra, dk_ref, dv_ref, wk_ref, wv_ref, *refs):
    out_refs = refs[len(extra) :]
    total = dot(dk_ref[...], wk_ref[...], NT) + dot(dv_ref[...], wv_ref[...], NT)
    rows = total.shape[0]
    for place, ref in zip(extra, refs):
        part = ref[...].astype(F32)
        if place == "low":
            total = total + jnp.concatenate([part, jnp.zeros_like(part)], axis=0)
        elif place == "high":
            total = total + jnp.concatenate([jnp.zeros_like(part), part], axis=0)
        else:
            total = total + part
    each = rows // len(out_refs)
    for n, out_ref in enumerate(out_refs):
        out_ref[...] = total[n * each : (n + 1) * each].astype(BF)


def pair_dot(dk, dv, key_weight, value_weight, extra, places, outs):
    rows, inner = dk.shape
    features = key_weight.shape[0]
    tile = 512
    d_spec = pl.BlockSpec((rows, inner), lambda i: (0, 0))
    w_spec = pl.BlockSpec((tile, inner), lambda i: (i, 0))

    def cols(height):
        return pl.BlockSpec((height, tile), lambda i: (0, i))

    return pl.pallas_call(
        functools.partial(pair_kernel, places),
        out_shape=[jax.ShapeDtypeStruct((rows // outs, features), BF)] * outs,
        grid=(features // tile,),
        in_specs=[d_spec, d_spec, w_spec, w_spec] + [cols(value.shape[0]) for value in extra],
        out_specs=[cols(rows // outs)] * outs,
        compiler_params=params(),
        cost_estimate=pl.CostEstimate(
            flops=4 * rows * inner * features,
            bytes_accessed=4 * (rows + inner) * features,
            transcendentals=0,
        ),
    )(dk, dv, key_weight, value_weight, *extra)


def read_rows(refs):
    return jnp.concatenate([ref[...].reshape(-1, ref.shape[-1]) for ref in refs], axis=0)


def softmax(q, k):
    scores = dot(q, k, NT) * HEAD ** (-0.5)
    exponent = jnp.exp(scores - jnp.max(scores, axis=-1, keepdims=True))
    return exponent / jnp.sum(exponent, axis=-1, keepdims=True)


def forward_kernel(count, q_ref, *refs):
    keys, values = read_rows(refs[:count]), read_rows(refs[count : 2 * count])
    out_ref = refs[-1]
    for h in range(q_ref.shape[1] // HEAD):
        cols = slice(h * HEAD, (h + 1) * HEAD)
        low = softmax(q_ref[:, cols], keys[:, cols]).astype(BF)
        out_ref[:, cols] = dot(low, values[:, cols], NN).astype(BF)


def backward_kernel(count, q_ref, d_ref, *refs):
    keys, values = read_rows(refs[:count]), read_rows(refs[count : 2 * count])
    dq_ref, dk_refs, dv_refs = refs[2 * count], refs[2 * count + 1 : 2 * count + 5], refs[2 * count + 5 :]
    for h in range(q_ref.shape[1] // HEAD):
        cols = slice(h * HEAD, (h + 1) * HEAD)
        q, d, k, v = q_ref[:, cols], d_ref[:, cols], keys[:, cols], values[:, cols]
        attention = softmax(q, k)
        d_attention = dot(d, v, NT)
        inner = jnp.sum(attention * d_attention, axis=-1, keepdims=True)
        d_scores = (attention * (d_attention - inner) * HEAD ** (-0.5)).astype(BF)
        dq_ref[:, cols] = dot(d_scores, k, NN).astype(BF)
        dk = dot(d_scores, q, TN).astype(BF)
        dv = dot(attention.astype(BF), d, TN).astype(BF)
        for n in range(SIDE):
            shape = dk_refs[n].shape[:3] + (HEAD,)
            rows = slice(n * SPAN, (n + 1) * SPAN)
            dk_refs[n][:, :, :, cols] = dk[rows].reshape(shape)
            dv_refs[n][:, :, :, cols] = dv[rows].reshape(shape)


def attention_specs(keys, cols):
    return [pl.BlockSpec((k.shape[0], 1, 16, cols), lambda c: (0, c, 0, 0)) for k in keys]


def attend(queries, keys, values):
    rows, cols = queries.shape
    q_spec = pl.BlockSpec((SPAN, cols), lambda c: (c, 0))
    kv = attention_specs(keys, cols)
    return pl.pallas_call(
        functools.partial(forward_kernel, len(keys)),
        out_shape=jax.ShapeDtypeStruct((rows, cols), BF),
        grid=(rows // SPAN,),
        in_specs=[q_spec] + kv + kv,
        out_specs=q_spec,
        compiler_params=params(),
        cost_estimate=pl.CostEstimate(
            flops=4 * rows * 256 * cols, bytes_accessed=6 * 1024 * cols, transcendentals=rows * 1024
        ),
    )(queries, *keys, *values)


def attend_back(queries, d_context, keys, values):
    rows, cols = queries.shape
    q_spec = pl.BlockSpec((SPAN, cols), lambda c: (c, 0))
    kv = attention_specs(keys, cols)
    group = jax.ShapeDtypeStruct((SIDE, rows // SPAN, 16, cols), BF)
    group_spec = pl.BlockSpec((SIDE, 1, 16, cols), lambda c: (0, c, 0, 0))
    out = pl.pallas_call(
        functools.partial(backward_kernel, len(keys)),
        out_shape=[jax.ShapeDtypeStruct((rows, cols), BF)] + [group] * 8,
        grid=(rows // SPAN,),
        in_specs=[q_spec, q_spec] + kv + kv,
        out_specs=[q_spec] + [group_spec] * 8,
        compiler_params=params(),
        cost_estimate=pl.CostEstimate(
            flops=12 * rows * 256 * cols, bytes_accessed=12 * 1024 * cols, transcendentals=rows * 1024
        ),
    )(queries, d_context, *keys, *values)
    return out[0], [g.reshape(-1, cols) for g in out[1:5]], [g.reshape(-1, cols) for g in out[5:]]


def on_device(
    hidden,
    query_weight,
    key_weight,
    value_weight,
    output_weight,
    neighbour_states,
    neighbour_slot,
    d_output,
):
    index = relative_index()
    features = key_weight.shape[0]
    local = neighbour_states.shape[2]
    cols = query_weight.shape[1]
    chunk = neighbour_states.shape[1] // ENC
    used = neighbour_slot.size
    slot_shard = neighbour_slot.reshape(-1) // SEQ

    def index_of(*places):
        return jnp.concatenate([index[k, a:b] for k, a, b in places])

    arrived = lax.all_to_all(
        neighbour_states.reshape(SEQ * ENC, chunk, local), AXES, split_axis=0, concat_axis=0, tiled=True
    )
    h0 = gather_short(hidden)
    d0 = gather_short(d_output)
    arrived = arrived.reshape(SEQ, ENC, chunk, local)
    picked = jnp.take(arrived, slot_shard, axis=1)
    picked = picked.transpose(1, 2, 0, 3).reshape(used * chunk, features)

    s0 = gather_short(picked)
    h1, h3 = gather_long(h0)
    s1, s3 = gather_long(s0)
    h2a, h2b = gather_last(h1, h3)
    s2a, s2b = gather_last(s1, s3)
    d1, d3 = gather_long(d0)

    queries = gathered_dot(index_of((0, 0, 4)), [h0], query_weight, True, None, F32)
    queries = gathered_dot(index_of((1, 0, 4), (3, 0, 4)), [h1, h3], query_weight, True, queries, F32)
    queries = gathered_dot(index_of((2, 0, 2), (2, 2, 4)), [h2a, h2b], query_weight, True, queries, BF)

    def project(group, weight):
        flat = group.reshape(-1, features)
        return dot(flat, weight, NN).astype(BF).reshape(group.shape[0], -1, 16, cols)

    groups = [s0, s1, s2a, s2b, s3]
    keys = [project(group, key_weight) for group in groups]
    values = [project(group, value_weight) for group in groups]

    context = attend(queries, keys, values)
    output = scatter_sum(index, context, output_weight, False)

    d2a, d2b = gather_last(d1, d3)
    d_context = gathered_dot(index_of((0, 0, 4)), [d0], output_weight, False, None, F32)
    d_context = gathered_dot(index_of((1, 0, 4), (3, 0, 4)), [d1, d3], output_weight, False, d_context, F32)
    d_context = gathered_dot(index_of((2, 0, 2), (2, 2, 4)), [d2a, d2b], output_weight, False, d_context, BF)

    d_queries, d_keys, d_values = attend_back(queries, d_context, keys, values)

    def pair(k, extra, places, outs):
        return pair_dot(d_keys[k], d_values[k], key_weight, value_weight, extra, places, outs)

    far_a, far_b = pair(2, [], (), 2)
    from_a, from_b = move_v(far_a, 1), move_v(far_b, -1)
    (g3,) = pair(3, [from_a], ("low",), 1)
    (g1,) = pair(1, [from_b], ("high",), 1)
    r3, r1 = move_v(g3, 1), move_v(g1, -1)
    summed = scatter_short(pair(0, [r3, r1], ("all", "all"), 4))

    d_hidden = scatter_sum(index, d_queries, query_weight, True)

    placing = lax.broadcasted_iota(jnp.int32, (ENC, used), 0) == slot_shard[None, :]
    spread = summed.reshape(used, chunk, SEQ, local).transpose(2, 0, 1, 3)
    rank = jnp.argmax(placing, axis=1)
    spread = jnp.take(spread, rank, axis=1)
    spread = jnp.where(jnp.any(placing, axis=1)[None, :, None, None], spread, 0)
    back = lax.all_to_all(
        spread.reshape(SEQ * ENC, chunk, local), AXES, split_axis=0, concat_axis=0, tiled=True
    )
    d_states = back.reshape(neighbour_states.shape)
    return (output, d_hidden, d_states)


def solution(mesh):
    in_specs = (
        P("seq", "enc"),
        P(None, "enc"),
        P(None, "enc"),
        P(None, "enc"),
        P("enc", None),
        P("enc", None, "seq"),
        P("seq", None),
        P("seq", "enc"),
    )
    out_specs = (P("seq", "enc"), P("seq", "enc"), P("enc", None, "seq"))
    return jax.shard_map(
        on_device, mesh=mesh, in_specs=in_specs, out_specs=out_specs, check_vma=False
    )
```

```python
import functools

import jax
import jax.numpy as jnp
from jax import lax
from jax.experimental import pallas as pl
from jax.experimental.pallas import tpu as pltpu
from jax.sharding import PartitionSpec as P

HEAD = 128
SPAN = 64
SEQ = 8
SIDE = 4
ENC = SIDE * SIDE
BF = jnp.bfloat16
F32 = jnp.float32
AXES = ("seq", "enc")
MIB = 1024 * 1024
NT = (((1,), (1,)), ((), ()))
NN = (((1,), (0,)), ((), ()))
TN = (((0,), (0,)), ((), ()))


def dot(a, b, dims):
    return lax.dot_general(a, b, dims, preferred_element_type=F32)


def shift_table(long_phase, shift):
    pairs = []
    for seq in range(SEQ):
        for z in range(SIDE):
            for x in range(SIDE):
                if (seq % 2 == 0) == long_phase:
                    to_z, to_x = (z + shift) % SIDE, x
                else:
                    to_z, to_x = z, (x + shift) % SIDE
                pairs.append((seq * ENC + z * SIDE + x, seq * ENC + to_z * SIDE + to_x))
    return pairs


def move_u(value, shift):
    return lax.ppermute(value, AXES, shift_table(False, shift))


def move_v(value, shift):
    return lax.ppermute(value, AXES, shift_table(True, shift))


def relative_index():
    seq, enc = lax.axis_index("seq"), lax.axis_index("enc")
    z, x = enc // SIDE, enc % SIDE
    even = seq % 2 == 0
    u, v = jnp.where(even, x, z), jnp.where(even, z, x)
    k = lax.broadcasted_iota(jnp.int32, (SIDE, SIDE), 0)
    j = lax.broadcasted_iota(jnp.int32, (SIDE, SIDE), 1)
    uu, vv = (u - j) % SIDE, (v - k) % SIDE
    return jnp.where(even, vv * SIDE + uu, uu * SIDE + vv).astype(jnp.int32)


def after(value, *others):
    return lax.optimization_barrier((value, *others))[0]


def stack_kernel(*refs):
    for n, ref in enumerate(refs[:-1]):
        refs[-1][n] = ref[...]


def stack(values):
    return pl.pallas_call(
        stack_kernel,
        out_shape=jax.ShapeDtypeStruct((len(values),) + values[0].shape, BF),
        in_specs=[pl.BlockSpec(memory_space=pltpu.VMEM)] * len(values),
        out_specs=pl.BlockSpec(memory_space=pltpu.VMEM),
        compiler_params=params(4),
        cost_estimate=cost(0, 4 * len(values) * values[0].size),
    )(*values)


def halves_kernel(one_ref, three_ref, low_ref, high_ref):
    low_ref[...] = one_ref[:2]
    high_ref[...] = three_ref[2:]


def halves(one, three):
    half = jax.ShapeDtypeStruct((2,) + one.shape[1:], BF)
    return pl.pallas_call(
        halves_kernel,
        out_shape=[half, half],
        in_specs=[pl.BlockSpec(memory_space=pltpu.VMEM)] * 2,
        out_specs=[pl.BlockSpec(memory_space=pltpu.VMEM)] * 2,
        compiler_params=params(4),
        cost_estimate=cost(0, 4 * one.size),
    )(one, three)


def gather_short(own):
    return [own, move_u(own, 1), move_u(own, 2), move_u(own, -1)]


def gather_long(group):
    return [move_v(group, 1), move_v(group, -1)]


def gather_last(side, *others):
    low, high = halves(*side)
    return [move_v(after(low, *others), 1), move_v(after(high, *others), -1)]


def params(mib):
    return pltpu.CompilerParams(vmem_limit_bytes=mib * MIB)


def in_vmem(count):
    return [pl.BlockSpec(memory_space=pltpu.VMEM)] * count


def cost(flops, bytes_accessed, transcendentals=0):
    return pl.CostEstimate(flops=flops, bytes_accessed=bytes_accessed, transcendentals=transcendentals)


DEPTH = 4


class Stream:
    def __init__(self, index_ref, count, query_ref, output_ref, scratch):
        self.index_ref, self.count = index_ref, count
        self.refs = (query_ref, output_ref)
        self.buffers, self.sems = scratch[:2], scratch[2:]
        for n in range(min(DEPTH - 1, count)):
            self.start(n)

    def copy(self, n, side):
        width = self.buffers[0].shape[1]
        at = pl.ds(pl.multiple_of(self.index_ref[n] * width, width), width)
        source = self.refs[0].at[at, :] if side == 0 else self.refs[1].at[:, at]
        slot = n % DEPTH
        return pltpu.make_async_copy(source, self.buffers[side].at[slot], self.sems[side].at[slot])

    def start(self, n):
        self.copy(n, 0).start()
        self.copy(n, 1).start()

    def blocks(self):
        for n in range(self.count):
            if n + DEPTH - 1 < self.count:
                self.start(n + DEPTH - 1)
            self.copy(n, 0).wait()
            self.copy(n, 1).wait()
            yield n, self.buffers[0].at[n % DEPTH], self.buffers[1].at[n % DEPTH]


def stream_scratch(width):
    return [
        pltpu.VMEM((DEPTH, width, width), BF),
        pltpu.VMEM((DEPTH, width, width), BF),
        pltpu.SemaphoreType.DMA((DEPTH,)),
        pltpu.SemaphoreType.DMA((DEPTH,)),
    ]


def in_hbm(count):
    return [pl.BlockSpec(memory_space=pltpu.HBM)] * count


def kept(*weights):
    return [pltpu.with_memory_space_constraint(weight, pltpu.HBM) for weight in weights]


def gathered_kernel(counts, has_start, index_ref, query_ref, output_ref, *refs):
    x_refs, refs = refs[: len(counts)], refs[len(counts) :]
    start_refs, refs = (refs[:2], refs[2:]) if has_start else (None, refs)
    (q_ref, d_ref), scratch = refs[:2], refs[2:]
    chunks = [x_ref.at[n] for count, x_ref in zip(counts, x_refs) for n in range(count)]
    q = start_refs[0][...] if has_start else None
    d = start_refs[1][...] if has_start else None
    for n, query_block, output_block in Stream(index_ref, len(chunks), query_ref, output_ref, scratch).blocks():
        term = dot(chunks[n][0], query_block[...], NN)
        q = term if q is None else q + term
        term = dot(chunks[n][1], output_block[...], NT)
        d = term if d is None else d + term
    q_ref[...] = q.astype(q_ref.dtype)
    d_ref[...] = d.astype(d_ref.dtype)


def gathered_dots(index, parts, query_weight, output_weight, start, out_type):
    rows, width = parts[0].shape[2:]
    cols = query_weight.shape[1]
    counts = [part.shape[0] for part in parts]
    count = sum(counts)
    return pl.pallas_call(
        functools.partial(gathered_kernel, counts, start is not None),
        out_shape=[jax.ShapeDtypeStruct((rows, cols), out_type)] * 2,
        in_specs=[pl.BlockSpec(memory_space=pltpu.SMEM)]
        + in_hbm(2)
        + in_vmem(len(parts) + (0 if start is None else 2)),
        out_specs=in_vmem(2),
        scratch_shapes=stream_scratch(width),
        compiler_params=params(10),
        cost_estimate=cost(4 * count * rows * width * cols, 4 * count * (rows + cols) * width),
    )(index, *kept(query_weight, output_weight), *parts, *([] if start is None else start))


def far_kernel(index_ref, query_ref, output_ref, c_ref, d_ref, low_ref, high_ref, *scratch):
    for n, query_block, output_block in Stream(index_ref, 4, query_ref, output_ref, scratch).blocks():
        out_ref = low_ref if n < 2 else high_ref
        out_ref[n % 2, 0] = dot(c_ref[...], output_block[...], NN).astype(BF)
        out_ref[n % 2, 1] = dot(d_ref[...], query_block[...], NT).astype(BF)


def side_kernel(index_ref, query_ref, output_ref, c_ref, d_ref, a_ref, b_ref, g3_ref, g1_ref, *scratch):
    for n, query_block, output_block in Stream(index_ref, 8, query_ref, output_ref, scratch).blocks():
        j = n % 4
        out_ref = g3_ref if n < 4 else g1_ref
        part_ref = None
        if n < 4 and j < 2:
            part_ref = a_ref.at[j]
        elif n >= 4 and j >= 2:
            part_ref = b_ref.at[j - 2]
        value = dot(c_ref[...], output_block[...], NN)
        if part_ref is not None:
            value = value + part_ref[0].astype(F32)
        out_ref[j, 0] = value.astype(BF)
        value = dot(d_ref[...], query_block[...], NT)
        if part_ref is not None:
            value = value + part_ref[1].astype(F32)
        out_ref[j, 1] = value.astype(BF)


def near_kernel(index_ref, query_ref, output_ref, c_ref, d_ref, r3_ref, r1_ref, *refs):
    t_refs, scratch = refs[:4], refs[4:]
    for n, query_block, output_block in Stream(index_ref, 4, query_ref, output_ref, scratch).blocks():
        value = dot(c_ref[...], output_block[...], NN)
        t_refs[n][0] = (value + r3_ref[n, 0].astype(F32) + r1_ref[n, 0].astype(F32)).astype(BF)
        value = dot(d_ref[...], query_block[...], NT)
        t_refs[n][1] = (value + r3_ref[n, 1].astype(F32) + r1_ref[n, 1].astype(F32)).astype(BF)


def scatter_sums(index, context, d_queries, query_weight, output_weight, *others):
    rows, inner = context.shape
    width = query_weight.shape[0] // ENC

    def call(kernel, place, extra, out_blocks):
        count = place.shape[0]
        return pl.pallas_call(
            kernel,
            out_shape=[jax.ShapeDtypeStruct(block + (2, rows, width), BF) for block in out_blocks],
            in_specs=[pl.BlockSpec(memory_space=pltpu.SMEM)] + in_hbm(2) + in_vmem(2 + len(extra)),
            out_specs=in_vmem(len(out_blocks)),
            scratch_shapes=stream_scratch(width),
            compiler_params=params(10),
            cost_estimate=cost(4 * count * rows * inner * width, 4 * count * (2 * rows + inner) * width),
        )(place, *kept(query_weight, output_weight), context, d_queries, *extra)

    context = after(context, *others)
    far_low, far_high = call(far_kernel, index[2], [], [(2,), (2,)])
    from_low, from_high = move_v(far_low, 1), move_v(far_high, -1)
    g3, g1 = call(
        side_kernel, jnp.concatenate([index[3], index[1]]), [from_low, from_high], [(4,), (4,)]
    )
    r3, r1 = move_v(g3, 1), move_v(g1, -1)
    pieces = call(near_kernel, index[0], [r3, r1], [()] * 4)
    total = scatter_short(pieces)
    return total[0], total[1], pieces


def scatter_short(pieces, *others):
    t0, t1, t2, t3 = pieces
    q1, q2, q3 = move_u(t1, -1), move_u(t2, 2), move_u(t3, 1)
    t0 = after(t0, *others)
    total = t0.astype(F32) + q1.astype(F32) + q2.astype(F32) + q3.astype(F32)
    return total.astype(BF)


def project_kernel(pairs, key_ref, value_ref, *refs):
    x_refs, (k_ref, v_ref) = refs[:pairs], refs[pairs:]
    x = jnp.concatenate([ref[...].reshape(-1, ref.shape[-1]) for ref in x_refs], axis=0)
    k_ref[...] = dot(x, key_ref[...], NN).astype(BF)
    v_ref[...] = dot(x, value_ref[...], NN).astype(BF)


def project(pairs, key_weight, value_weight):
    features, cols = key_weight.shape
    rows = sum(pair.shape[0] * pair.shape[1] for pair in pairs)
    return pl.pallas_call(
        functools.partial(project_kernel, len(pairs)),
        out_shape=[jax.ShapeDtypeStruct((rows, cols), BF)] * 2,
        in_specs=in_vmem(2 + len(pairs)),
        out_specs=in_vmem(2),
        compiler_params=params(8),
        cost_estimate=cost(4 * rows * features * cols, 4 * (rows + cols) * features),
    )(key_weight, value_weight, *pairs)


def pair_kernel(places, groups, key_ref, value_ref, *refs):
    count = 2 * groups
    d_refs, refs = refs[:count], refs[count:]
    extra_refs, out_refs = refs[: len(places)], refs[len(places) :]
    tile = key_ref.shape[1]
    rows = d_refs[0].shape[0]
    per_group = len(out_refs) // groups
    each = rows // per_group
    for n in range(key_ref.shape[0] // tile):
        cols = slice(n * tile, (n + 1) * tile)
        for g in range(groups):
            total = dot(d_refs[2 * g][...], key_ref[cols, :], NT)
            total = total + dot(d_refs[2 * g + 1][...], value_ref[cols, :], NT)
            for (group, first, size), extra_ref in zip(places, extra_refs):
                if group != g:
                    continue
                part = extra_ref[:, cols].astype(F32)
                if size < rows:
                    zero = jnp.zeros((rows - size, tile), F32)
                    part = jnp.concatenate([zero, part] if first else [part, zero], axis=0)
                total = total + part
            for m in range(per_group):
                out_refs[g * per_group + m][:, cols] = total[m * each : (m + 1) * each].astype(BF)


def pair_dots(grads, key_weight, value_weight, extra, places, per_group):
    groups = len(grads) // 2
    rows, inner = grads[0].shape
    features = key_weight.shape[0]
    return pl.pallas_call(
        functools.partial(pair_kernel, places, groups),
        out_shape=[jax.ShapeDtypeStruct((rows // per_group, features), BF)] * (groups * per_group),
        in_specs=in_vmem(2 + len(grads) + len(extra)),
        out_specs=in_vmem(groups * per_group),
        compiler_params=params(8),
        cost_estimate=cost(4 * groups * rows * inner * features, 4 * (groups * rows + inner) * features),
    )(key_weight, value_weight, *grads, *extra)


def attention_kernel(chunks, q_ref, d_ref, *refs):
    parts = len(chunks)
    keys, values = refs[:parts], refs[parts : 2 * parts]
    context_ref, dq_ref = refs[2 * parts : 2 * parts + 2]
    dk_refs, dv_refs = refs[2 * parts + 2 : 2 * parts + 6], refs[2 * parts + 6 :]
    scale = HEAD ** (-0.5)
    spans = q_ref.shape[0] // SPAN
    own = 256 // ENC
    places = [(part, n * spans * own) for part, count in enumerate(chunks) for n in range(count)]

    def span_rows(refs, c, cols):
        return jnp.concatenate([refs[part][at + c * own : at + (c + 1) * own, cols] for part, at in places], axis=0)

    for c in range(spans):
        rows = slice(c * SPAN, (c + 1) * SPAN)
        heads = [slice(h * HEAD, (h + 1) * HEAD) for h in range(q_ref.shape[1] // HEAD)]
        q, d = [q_ref[rows, cols] for cols in heads], [d_ref[rows, cols] for cols in heads]
        k, v = [span_rows(keys, c, cols) for cols in heads], [span_rows(values, c, cols) for cols in heads]
        scores = [dot(a, b, NT) * scale for a, b in zip(q, k)]
        d_attention = [dot(a, b, NT) for a, b in zip(d, v)]
        exponent = [jnp.exp(a - jnp.max(a, axis=-1, keepdims=True)) for a in scores]
        attention = [a * (1.0 / jnp.sum(a, axis=-1, keepdims=True)) for a in exponent]
        low = [a.astype(BF) for a in attention]
        inner = [jnp.sum(a * b, axis=-1, keepdims=True) for a, b in zip(attention, d_attention)]
        d_scores = [
            (a * (b - c) * scale).astype(BF) for a, b, c in zip(attention, d_attention, inner)
        ]
        for h, cols in enumerate(heads):
            context_ref[rows, cols] = dot(low[h], v[h], NN).astype(BF)
            dq_ref[rows, cols] = dot(d_scores[h], k[h], NN).astype(BF)
        for h, cols in enumerate(heads):
            dk = dot(d_scores[h], q[h], TN).astype(BF)
            dv = dot(low[h], d[h], TN).astype(BF)
            for n in range(ENC):
                at = (n % SIDE) * spans * own + c * own
                dk_refs[n // SIDE][at : at + own, cols] = dk[n * own : (n + 1) * own]
                dv_refs[n // SIDE][at : at + own, cols] = dv[n * own : (n + 1) * own]


def attend(queries, d_context, keys, values):
    rows, cols = queries.shape
    group_rows = sum(k.shape[0] for k in keys) // SIDE
    chunks = [k.shape[0] * ENC // (SIDE * group_rows) for k in keys]
    row_out = jax.ShapeDtypeStruct((rows, cols), BF)
    group = jax.ShapeDtypeStruct((group_rows, cols), BF)
    out = pl.pallas_call(
        functools.partial(attention_kernel, chunks),
        out_shape=[row_out] * 2 + [group] * 8,
        in_specs=in_vmem(2 + 2 * len(keys)),
        out_specs=in_vmem(10),
        compiler_params=params(8),
        cost_estimate=cost(12 * rows * 256 * cols, 20 * 1024 * cols, rows * 1024),
    )(queries, d_context, *keys, *values)
    return out[0], out[1], out[2:6], out[6:]


def on_device(
    hidden,
    query_weight,
    key_weight,
    value_weight,
    output_weight,
    neighbour_states,
    neighbour_slot,
    d_output,
):
    index = relative_index()
    features = key_weight.shape[0]
    local = neighbour_states.shape[2]
    chunk = neighbour_states.shape[1] // ENC
    used = neighbour_slot.size
    slot_shard = neighbour_slot.reshape(-1) // SEQ

    near = gather_short(stack([hidden, d_output]))
    arrived = lax.all_to_all(
        neighbour_states.reshape(SEQ * ENC, chunk, local), AXES, split_axis=0, concat_axis=0, tiled=True
    )
    near = stack([after(near[0], arrived)] + near[1:])
    side = gather_long(near)
    arrived = arrived.reshape(SEQ, ENC, chunk, local)
    picked = jnp.take(arrived, slot_shard, axis=1)
    picked = picked.transpose(1, 2, 0, 3).reshape(used * chunk, features)
    state_near = stack(gather_short(picked))
    state_side = gather_long(state_near)

    q_d = gathered_dots(index[0], [near], query_weight, output_weight, None, F32)
    kv_near = project([state_near], key_weight, value_weight)
    far = gather_last(side, *q_d)
    q_d = gathered_dots(
        jnp.concatenate([index[1], index[3]]), side, query_weight, output_weight, q_d, F32
    )
    state_far = gather_last(state_side, *q_d, *kv_near)
    kv_side = project(state_side, key_weight, value_weight)
    queries, d_context = gathered_dots(index[2], far, query_weight, output_weight, q_d, BF)
    state_far[0] = after(state_far[0], queries, *kv_side)
    kv_far = project(state_far, key_weight, value_weight)
    keys, values = zip(kv_near, kv_side, kv_far)

    context, d_queries, d_keys, d_values = attend(queries, d_context, keys, values)
    grads = {k: [d_keys[n], d_values[n]] for n, k in enumerate((0, 1, 3, 2))}

    def pair(groups, extra, places, outs):
        return pair_dots(sum((grads[k] for k in groups), []), key_weight, value_weight, extra, places, outs)

    half, whole = grads[0][0].shape[0] // 2, grads[0][0].shape[0]
    far_low, far_high = pair([2], [], (), 2)
    from_low, from_high = move_v(far_low, 1), move_v(far_high, -1)
    g3, g1 = pair([3, 1], [from_low, from_high], ((0, 0, half), (1, half, half)), 1)
    r3, r1 = move_v(g3, 1), move_v(g1, -1)
    output, d_hidden, pieces = scatter_sums(index, context, d_queries, query_weight, output_weight, far_low)
    summed = scatter_short(pair([0], [r3, r1], ((0, 0, whole), (0, 0, whole)), 4), *pieces)

    placing = lax.broadcasted_iota(jnp.int32, (ENC, used), 0) == slot_shard[None, :]
    spread = summed.reshape(used, chunk, SEQ, local).transpose(2, 0, 1, 3)
    rank = jnp.argmax(placing, axis=1)
    spread = jnp.take(spread, rank, axis=1)
    spread = jnp.where(jnp.any(placing, axis=1)[None, :, None, None], spread, 0)
    back = lax.all_to_all(
        spread.reshape(SEQ * ENC, chunk, local), AXES, split_axis=0, concat_axis=0, tiled=True
    )
    d_states = back.reshape(neighbour_states.shape)
    return (output, d_hidden, d_states)


def solution(mesh):
    in_specs = (
        P("seq", "enc"),
        P(None, "enc"),
        P(None, "enc"),
        P(None, "enc"),
        P("enc", None),
        P("enc", None, "seq"),
        P("seq", None),
        P("seq", "enc"),
    )
    out_specs = (P("seq", "enc"), P("seq", "enc"), P("enc", None, "seq"))
    return jax.shard_map(
        on_device, mesh=mesh, in_specs=in_specs, out_specs=out_specs, check_vma=False
    )
```

```python
import functools

import jax
import jax.numpy as jnp
from jax import lax
from jax.experimental import pallas as pl
from jax.experimental.pallas import tpu as pltpu
from jax.sharding import PartitionSpec as P

HEAD = 128
SPAN = 64
SEQ = 8
SIDE = 4
ENC = SIDE * SIDE
BF = jnp.bfloat16
F32 = jnp.float32
AXES = ("seq", "enc")
MIB = 1024 * 1024
NT = (((1,), (1,)), ((), ()))
NN = (((1,), (0,)), ((), ()))
TN = (((0,), (0,)), ((), ()))


def dot(a, b, dims):
    return lax.dot_general(a, b, dims, preferred_element_type=F32)


def shift_table(long_phase, shift):
    pairs = []
    for seq in range(SEQ):
        for z in range(SIDE):
            for x in range(SIDE):
                if (seq % 2 == 0) == long_phase:
                    to_z, to_x = (z + shift) % SIDE, x
                else:
                    to_z, to_x = z, (x + shift) % SIDE
                pairs.append((seq * ENC + z * SIDE + x, seq * ENC + to_z * SIDE + to_x))
    return pairs


def move_u(value, shift):
    return lax.ppermute(value, AXES, shift_table(False, shift))


def move_v(value, shift):
    return lax.ppermute(value, AXES, shift_table(True, shift))


def relative_index():
    seq, enc = lax.axis_index("seq"), lax.axis_index("enc")
    z, x = enc // SIDE, enc % SIDE
    even = seq % 2 == 0
    u, v = jnp.where(even, x, z), jnp.where(even, z, x)
    k = lax.broadcasted_iota(jnp.int32, (SIDE, SIDE), 0)
    j = lax.broadcasted_iota(jnp.int32, (SIDE, SIDE), 1)
    uu, vv = (u - j) % SIDE, (v - k) % SIDE
    return jnp.where(even, vv * SIDE + uu, uu * SIDE + vv).astype(jnp.int32)


def after(value, *others):
    return lax.optimization_barrier((value, *others))[0]


def stack_kernel(*refs):
    for n, ref in enumerate(refs[:-1]):
        refs[-1][n] = ref[...]


def stack(values):
    return pl.pallas_call(
        stack_kernel,
        out_shape=jax.ShapeDtypeStruct((len(values),) + values[0].shape, BF),
        in_specs=[pl.BlockSpec(memory_space=pltpu.VMEM)] * len(values),
        out_specs=pl.BlockSpec(memory_space=pltpu.VMEM),
        compiler_params=params(8),
        cost_estimate=cost(0, 4 * len(values) * values[0].size),
    )(*values)


def join_kernel(one_ref, two_ref, out_ref, sems):
    copies = [pltpu.make_async_copy(ref, out_ref.at[n], sems.at[n]) for n, ref in enumerate((one_ref, two_ref))]
    for copy in copies:
        copy.start()
    for copy in copies:
        copy.wait()


def join(one, two):
    return pl.pallas_call(
        join_kernel,
        out_shape=jax.ShapeDtypeStruct((2,) + one.shape, BF),
        in_specs=in_hbm(2),
        out_specs=pl.BlockSpec(memory_space=pltpu.VMEM),
        scratch_shapes=[pltpu.SemaphoreType.DMA((2,))],
        compiler_params=params(8),
        cost_estimate=cost(0, 8 * one.size),
    )(*kept(one, two))


def halves_kernel(one_ref, three_ref, low_ref, high_ref):
    low_ref[...] = one_ref[:2]
    high_ref[...] = three_ref[2:]


def halves(one, three):
    half = jax.ShapeDtypeStruct((2,) + one.shape[1:], BF)
    return pl.pallas_call(
        halves_kernel,
        out_shape=[half, half],
        in_specs=[pl.BlockSpec(memory_space=pltpu.VMEM)] * 2,
        out_specs=[pl.BlockSpec(memory_space=pltpu.VMEM)] * 2,
        compiler_params=params(8),
        cost_estimate=cost(0, 4 * one.size),
    )(one, three)


def gather_short(own):
    return [own, move_u(own, 1), move_u(own, 2), move_u(own, -1)]


def gather_long(group):
    return [move_v(group, 1), move_v(group, -1)]


def gather_last(side, *others):
    low, high = halves(*side)
    return [move_v(after(low, *others), 1), move_v(after(high, *others), -1)]


def params(mib):
    return pltpu.CompilerParams(vmem_limit_bytes=mib * MIB)


def in_vmem(count):
    return [pl.BlockSpec(memory_space=pltpu.VMEM)] * count


def cost(flops, bytes_accessed, transcendentals=0):
    return pl.CostEstimate(flops=flops // 1024, bytes_accessed=bytes_accessed // 1024, transcendentals=0)


DEPTH = 4


class Stream:
    def __init__(self, index_ref, count, query_ref, output_ref, scratch):
        self.index_ref, self.count = index_ref, count
        self.refs = (query_ref, output_ref)
        self.buffers, self.sems = scratch[:2], scratch[2:]
        for n in range(min(DEPTH - 1, count)):
            self.start(n)

    def copy(self, n, side):
        width = self.buffers[0].shape[1]
        at = pl.ds(pl.multiple_of(self.index_ref[n] * width, width), width)
        source = self.refs[0].at[at, :] if side == 0 else self.refs[1].at[:, at]
        slot = n % DEPTH
        return pltpu.make_async_copy(source, self.buffers[side].at[slot], self.sems[side].at[slot])

    def start(self, n):
        self.copy(n, 0).start()
        self.copy(n, 1).start()

    def blocks(self):
        for n in range(self.count):
            if n + DEPTH - 1 < self.count:
                self.start(n + DEPTH - 1)
            self.copy(n, 0).wait()
            self.copy(n, 1).wait()
            yield n, self.buffers[0].at[n % DEPTH], self.buffers[1].at[n % DEPTH]


def stream_scratch(width):
    return [
        pltpu.VMEM((DEPTH, width, width), BF),
        pltpu.VMEM((DEPTH, width, width), BF),
        pltpu.SemaphoreType.DMA((DEPTH,)),
        pltpu.SemaphoreType.DMA((DEPTH,)),
    ]


def in_hbm(count):
    return [pl.BlockSpec(memory_space=pltpu.HBM)] * count


def kept(*weights):
    return [pltpu.with_memory_space_constraint(weight, pltpu.HBM) for weight in weights]


def gathered_kernel(counts, has_start, index_ref, query_ref, output_ref, *refs):
    x_refs, refs = refs[: len(counts)], refs[len(counts) :]
    start_refs, refs = (refs[:2], refs[2:]) if has_start else (None, refs)
    (q_ref, d_ref), scratch = refs[:2], refs[2:]
    chunks = [x_ref.at[n] for count, x_ref in zip(counts, x_refs) for n in range(count)]
    q = start_refs[0][...] if has_start else None
    d = start_refs[1][...] if has_start else None
    for n, query_block, output_block in Stream(index_ref, len(chunks), query_ref, output_ref, scratch).blocks():
        term = dot(chunks[n][0], query_block[...], NN)
        q = term if q is None else q + term
        term = dot(chunks[n][1], output_block[...], NT)
        d = term if d is None else d + term
    q_ref[...] = q.astype(q_ref.dtype)
    d_ref[...] = d.astype(d_ref.dtype)


def gathered_dots(index, parts, query_weight, output_weight, start, out_type):
    rows, width = parts[0].shape[2:]
    cols = query_weight.shape[1]
    counts = [part.shape[0] for part in parts]
    count = sum(counts)
    return pl.pallas_call(
        functools.partial(gathered_kernel, counts, start is not None),
        out_shape=[jax.ShapeDtypeStruct((rows, cols), out_type)] * 2,
        in_specs=[pl.BlockSpec(memory_space=pltpu.SMEM)]
        + in_hbm(2)
        + in_vmem(len(parts) + (0 if start is None else 2)),
        out_specs=in_vmem(2),
        scratch_shapes=stream_scratch(width),
        compiler_params=params(8),
        cost_estimate=cost(4 * count * rows * width * cols, 4 * count * (rows + cols) * width),
    )(index, *kept(query_weight, output_weight), *parts, *([] if start is None else start))


def terms_kernel(count, index_ref, query_ref, output_ref, c_ref, d_ref, *refs):
    out_refs, scratch = refs[:-4], refs[-4:]
    targets = [(ref, at) for ref in out_refs for at in range(0, ref.shape[0], 2)]
    for n, query_block, output_block in Stream(index_ref, count, query_ref, output_ref, scratch).blocks():
        out_ref, at = targets[n]
        out_ref[at] = dot(c_ref[...], output_block[...], NN).astype(BF)
        out_ref[at + 1] = dot(d_ref[...], query_block[...], NT).astype(BF)


def scatter_terms(context, d_queries, query_weight, output_weight):
    rows, inner = context.shape
    width = query_weight.shape[0] // ENC

    def call(place, out_tiles, *others):
        count = place.shape[0]
        return pl.pallas_call(
            functools.partial(terms_kernel, count),
            out_shape=[jax.ShapeDtypeStruct((tiles, rows, width), BF) for tiles in out_tiles],
            in_specs=[pl.BlockSpec(memory_space=pltpu.SMEM)] + in_hbm(2) + in_vmem(2),
            out_specs=in_vmem(len(out_tiles)),
            scratch_shapes=stream_scratch(width),
            compiler_params=params(8),
            cost_estimate=cost(4 * count * rows * inner * width, 4 * count * (2 * rows + inner) * width),
        )(place, *kept(query_weight, output_weight), after(context, *others), d_queries)

    return call


def plus(*values):
    return sum(value.astype(F32) for value in values).astype(BF)


def pass_on_kernel(g3_ref, g1_ref, low_ref, high_ref, far_low_ref, far_high_ref, up_ref, down_ref):
    for n in range(2):
        up_ref[n] = plus(g3_ref[n], low_ref[n])
        up_ref[n + 2] = g3_ref[n + 2]
        down_ref[n] = g1_ref[n]
        down_ref[n + 2] = plus(g1_ref[n + 2], high_ref[n])
    for n in range(4):
        up_ref[n + 4] = far_low_ref[n]
        down_ref[n + 4] = far_high_ref[n]


def pass_on(g3, g1, low, high, far_low, far_high):
    return pl.pallas_call(
        pass_on_kernel,
        out_shape=[jax.ShapeDtypeStruct((8,) + g3.shape[1:], BF)] * 2,
        in_specs=in_vmem(6),
        out_specs=in_vmem(2),
        compiler_params=params(8),
        cost_estimate=cost(g3.size, 8 * g3.size),
    )(g3, g1, low, high, far_low, far_high)


def add_halves_kernel(g3_ref, g1_ref, up_ref, down_ref, out3_ref, out1_ref):
    for n in range(4):
        out3_ref[n] = plus(g3_ref[n], up_ref[n + 4])
        out3_ref[n + 4] = g3_ref[n + 4]
        out1_ref[n] = g1_ref[n]
        out1_ref[n + 4] = plus(g1_ref[n + 4], down_ref[n + 4])


def add_halves(g3, g1, up, down):
    return pl.pallas_call(
        add_halves_kernel,
        out_shape=[jax.ShapeDtypeStruct(g3.shape, BF)] * 2,
        in_specs=in_vmem(4),
        out_specs=in_vmem(2),
        compiler_params=params(8),
        cost_estimate=cost(g3.size, 4 * g3.size),
    )(g3, g1, up, down)


def add_pieces_kernel(*refs):
    r3_ref, r1_ref = refs[4:6]
    for n in range(4):
        tiles = refs[n].shape[0]
        for m in range(tiles):
            refs[6 + n][m] = plus(refs[n][m], r3_ref[n * tiles + m], r1_ref[n * tiles + m])


def add_pieces(pieces, r3, r1):
    return pl.pallas_call(
        add_pieces_kernel,
        out_shape=[jax.ShapeDtypeStruct(pieces[0].shape, BF)] * 4,
        in_specs=in_vmem(6),
        out_specs=in_vmem(4),
        compiler_params=params(8),
        cost_estimate=cost(8 * r3.size, 8 * r3.size),
    )(*pieces, r3, r1)


def move_pieces(pieces):
    return move_u(pieces[1], -1), move_u(pieces[2], 2), move_u(pieces[3], 1)


def finish_kernel(*refs):
    for n, ref in enumerate(refs[4:]):
        ref[...] = plus(*[part[n] for part in refs[:4]])


def finish(*parts):
    tiles = parts[0].shape[0]
    return pl.pallas_call(
        finish_kernel,
        out_shape=[jax.ShapeDtypeStruct(parts[0].shape[1:], BF)] * tiles,
        in_specs=in_vmem(4),
        out_specs=in_vmem(tiles),
        compiler_params=params(8),
        cost_estimate=cost(4 * parts[0].size, 10 * parts[0].size),
    )(*parts)


def project_kernel(pairs, key_ref, value_ref, *refs):
    x_refs, (k_ref, v_ref) = refs[:pairs], refs[pairs:]
    x = jnp.concatenate([ref[...].reshape(-1, ref.shape[-1]) for ref in x_refs], axis=0)
    k_ref[...] = dot(x, key_ref[...], NN).astype(BF)
    v_ref[...] = dot(x, value_ref[...], NN).astype(BF)


def project(pairs, key_weight, value_weight):
    features, cols = key_weight.shape
    rows = sum(pair.shape[0] * pair.shape[1] for pair in pairs)
    return pl.pallas_call(
        functools.partial(project_kernel, len(pairs)),
        out_shape=[jax.ShapeDtypeStruct((rows, cols), BF)] * 2,
        in_specs=in_vmem(2 + len(pairs)),
        out_specs=in_vmem(2),
        compiler_params=params(8),
        cost_estimate=cost(4 * rows * features * cols, 4 * (rows + cols) * features),
    )(key_weight, value_weight, *pairs)


def pair_kernel(groups, key_ref, value_ref, *refs):
    d_refs, out_refs = refs[: 2 * groups], refs[2 * groups :]
    tile = key_ref.shape[1]
    rows = d_refs[0].shape[0] // SIDE
    for n in range(key_ref.shape[0] // tile):
        targets = [(ref, m) for ref in out_refs for m in range(ref.shape[0])]
        for g in range(groups):
            total = dot(d_refs[2 * g][...], key_ref[n * tile : (n + 1) * tile, :], NT)
            total = (total + dot(d_refs[2 * g + 1][...], value_ref[n * tile : (n + 1) * tile, :], NT)).astype(BF)
            for m in range(SIDE):
                out_ref, at = targets[g * SIDE + m]
                out_ref[at, n * rows : (n + 1) * rows, :] = total[m * rows : (m + 1) * rows]


def pair_dots(grads, key_weight, value_weight, outs):
    rows, inner = grads[0].shape
    features = key_weight.shape[0]
    shape = (rows // SIDE * (features // inner), inner)
    groups = len(grads) // 2
    return pl.pallas_call(
        functools.partial(pair_kernel, groups),
        out_shape=[jax.ShapeDtypeStruct((chunks,) + shape, BF) for chunks in outs],
        in_specs=in_vmem(2 + len(grads)),
        out_specs=in_vmem(len(outs)),
        compiler_params=params(8),
        cost_estimate=cost(4 * groups * rows * inner * features, 4 * (groups * rows + inner) * features),
    )(key_weight, value_weight, *grads)


def attention_kernel(chunks, q_ref, d_ref, *refs):
    parts = len(chunks)
    keys, values = refs[:parts], refs[parts : 2 * parts]
    context_ref, dq_ref = refs[2 * parts : 2 * parts + 2]
    dk_refs, dv_refs = refs[2 * parts + 2 : 2 * parts + 6], refs[2 * parts + 6 :]
    scale = HEAD ** (-0.5)
    spans = q_ref.shape[0] // SPAN
    own = 256 // ENC
    places = [(part, n * spans * own) for part, count in enumerate(chunks) for n in range(count)]

    def span_rows(refs, c, cols):
        return jnp.concatenate([refs[part][at + c * own : at + (c + 1) * own, cols] for part, at in places], axis=0)

    for c in range(spans):
        rows = slice(c * SPAN, (c + 1) * SPAN)
        heads = [slice(h * HEAD, (h + 1) * HEAD) for h in range(q_ref.shape[1] // HEAD)]
        q, d = [q_ref[rows, cols] for cols in heads], [d_ref[rows, cols] for cols in heads]
        k, v = [span_rows(keys, c, cols) for cols in heads], [span_rows(values, c, cols) for cols in heads]
        scores = [dot(a, b, NT) * scale for a, b in zip(q, k)]
        d_attention = [dot(a, b, NT) for a, b in zip(d, v)]
        exponent = [jnp.exp(a - jnp.max(a, axis=-1, keepdims=True)) for a in scores]
        attention = [a * (1.0 / jnp.sum(a, axis=-1, keepdims=True)) for a in exponent]
        low = [a.astype(BF) for a in attention]
        inner = [jnp.sum(a * b, axis=-1, keepdims=True) for a, b in zip(attention, d_attention)]
        d_scores = [
            (a * (b - c) * scale).astype(BF) for a, b, c in zip(attention, d_attention, inner)
        ]
        for h, cols in enumerate(heads):
            context_ref[rows, cols] = dot(low[h], v[h], NN).astype(BF)
            dq_ref[rows, cols] = dot(d_scores[h], k[h], NN).astype(BF)
        for h, cols in enumerate(heads):
            dk = dot(d_scores[h], q[h], TN).astype(BF)
            dv = dot(low[h], d[h], TN).astype(BF)
            for n in range(ENC):
                at = (n % SIDE) * spans * own + c * own
                dk_refs[n // SIDE][at : at + own, cols] = dk[n * own : (n + 1) * own]
                dv_refs[n // SIDE][at : at + own, cols] = dv[n * own : (n + 1) * own]


def attend(queries, d_context, keys, values):
    rows, cols = queries.shape
    group_rows = sum(k.shape[0] for k in keys) // SIDE
    chunks = [k.shape[0] * ENC // (SIDE * group_rows) for k in keys]
    row_out = jax.ShapeDtypeStruct((rows, cols), BF)
    group = jax.ShapeDtypeStruct((group_rows, cols), BF)
    out = pl.pallas_call(
        functools.partial(attention_kernel, chunks),
        out_shape=[row_out] * 2 + [group] * 8,
        in_specs=in_vmem(2 + 2 * len(keys)),
        out_specs=in_vmem(10),
        compiler_params=params(8),
        cost_estimate=cost(12 * rows * 256 * cols, 20 * 1024 * cols, rows * 1024),
    )(queries, d_context, *keys, *values)
    return out[0], out[1], out[2:6], out[6:]


def on_device(
    hidden,
    query_weight,
    key_weight,
    value_weight,
    output_weight,
    neighbour_states,
    neighbour_slot,
    d_output,
):
    index = relative_index()
    features, cols = key_weight.shape
    local = neighbour_states.shape[2]
    chunk = neighbour_states.shape[1] // ENC
    used = neighbour_slot.size
    slot_shard = neighbour_slot.reshape(-1) // SEQ

    near = gather_short(join(hidden, d_output))
    arrived = lax.all_to_all(
        neighbour_states.reshape(SEQ * ENC, chunk, local), AXES, split_axis=0, concat_axis=0, tiled=True
    )
    near = stack([after(near[0], arrived)] + near[1:])
    side = gather_long(near)
    arrived = arrived.reshape(SEQ, ENC, chunk, local)
    picked = jnp.take(arrived, slot_shard, axis=1)
    picked = picked.transpose(1, 2, 0, 3).reshape(used * chunk, features)
    state_near = stack(gather_short(picked))
    state_side = gather_long(state_near)

    q_d = gathered_dots(index[0], [near], query_weight, output_weight, None, F32)
    kv_near = project([state_near], key_weight, value_weight)
    far = gather_last(side, *q_d)
    q_d = gathered_dots(
        jnp.concatenate([index[1], index[3]]), side, query_weight, output_weight, q_d, F32
    )
    state_far = gather_last(state_side, *q_d, *kv_near)
    kv_side = project(state_side, key_weight, value_weight)
    queries, d_context = gathered_dots(index[2], far, query_weight, output_weight, q_d, BF)
    state_far[0] = after(state_far[0], queries, *kv_side)
    kv_far = project(state_far, key_weight, value_weight)
    keys, values = zip(kv_near, kv_side, kv_far)

    context, d_queries, d_keys, d_values = attend(queries, d_context, keys, values)
    grads = {k: [d_keys[n], d_values[n]] for n, k in enumerate((0, 1, 3, 2))}

    both_terms = scatter_terms(context, d_queries, query_weight, output_weight)
    far = pair_dots(grads[2], key_weight, value_weight, [2, 2])
    from_low, from_high = move_v(far[0], 1), move_v(far[1], -1)
    both_far = both_terms(index[2], [4, 4], far[0])
    grads[3][0] = after(grads[3][0], *both_far)
    rest = pair_dots(grads[3] + grads[1] + grads[0], key_weight, value_weight, [4, 4, 1, 1, 1, 1])
    up, down = pass_on(rest[0], rest[1], from_low, from_high, *both_far)
    from_up, from_down = move_v(up, 1), move_v(down, -1)
    both_side = both_terms(jnp.concatenate([index[3], index[1]]), [8, 8], up)
    g3, g1 = add_halves(*both_side, from_up, from_down)
    both_near = both_terms(index[0], [2] * 4, g3)
    r3, r1 = move_v(g3, 1), move_v(g1, -1)
    pieces = add_pieces(rest[2:], from_up, from_down)
    (summed,) = finish(pieces[0], *move_pieces(pieces))
    both_pieces = add_pieces(both_near, after(r3, summed), r1)
    output, d_hidden = finish(both_pieces[0], *move_pieces(both_pieces))

    placing = lax.broadcasted_iota(jnp.int32, (ENC, used), 0) == slot_shard[None, :]
    spread = summed.reshape(-1, used, chunk, cols // local, local).transpose(0, 3, 1, 2, 4)
    spread = spread.reshape(SEQ, used, chunk, local)
    rank = jnp.argmax(placing, axis=1)
    spread = jnp.take(spread, rank, axis=1)
    spread = jnp.where(jnp.any(placing, axis=1)[None, :, None, None], spread, 0)
    back = lax.all_to_all(
        after(spread, *both_pieces).reshape(SEQ * ENC, chunk, local), AXES, split_axis=0, concat_axis=0, tiled=True
    )
    d_states = back.reshape(neighbour_states.shape)
    return (output, d_hidden, d_states)


def solution(mesh):
    in_specs = (
        P("seq", "enc"),
        P(None, "enc"),
        P(None, "enc"),
        P(None, "enc"),
        P("enc", None),
        P("enc", None, "seq"),
        P("seq", None),
        P("seq", "enc"),
    )
    out_specs = (P("seq", "enc"), P("seq", "enc"), P("enc", None, "seq"))
    return jax.shard_map(
        on_device, mesh=mesh, in_specs=in_specs, out_specs=out_specs, check_vma=False
    )
```

```python
import functools

import jax
import jax.numpy as jnp
from jax import lax
from jax.experimental import pallas as pl
from jax.experimental.pallas import tpu as pltpu
from jax.sharding import PartitionSpec as P

HEAD = 128
SPAN = 64
SEQ = 8
SIDE = 4
ENC = SIDE * SIDE
BF = jnp.bfloat16
F32 = jnp.float32
AXES = ("seq", "enc")
MIB = 1024 * 1024
NT = (((1,), (1,)), ((), ()))
NN = (((1,), (0,)), ((), ()))
TN = (((0,), (0,)), ((), ()))


def dot(a, b, dims):
    return lax.dot_general(a, b, dims, preferred_element_type=F32)


def shift_table(long_phase, shift):
    pairs = []
    for seq in range(SEQ):
        for z in range(SIDE):
            for x in range(SIDE):
                if (seq % 2 == 0) == long_phase:
                    to_z, to_x = (z + shift) % SIDE, x
                else:
                    to_z, to_x = z, (x + shift) % SIDE
                pairs.append((seq * ENC + z * SIDE + x, seq * ENC + to_z * SIDE + to_x))
    return pairs


def move_u(value, shift):
    return lax.ppermute(value, AXES, shift_table(False, shift))


def move_v(value, shift):
    return lax.ppermute(value, AXES, shift_table(True, shift))


def relative_index():
    seq, enc = lax.axis_index("seq"), lax.axis_index("enc")
    z, x = enc // SIDE, enc % SIDE
    even = seq % 2 == 0
    u, v = jnp.where(even, x, z), jnp.where(even, z, x)
    k = lax.broadcasted_iota(jnp.int32, (SIDE, SIDE), 0)
    j = lax.broadcasted_iota(jnp.int32, (SIDE, SIDE), 1)
    uu, vv = (u - j) % SIDE, (v - k) % SIDE
    return jnp.where(even, vv * SIDE + uu, uu * SIDE + vv).astype(jnp.int32)


def after(value, *others):
    return lax.optimization_barrier((value, *others))[0]


def stack_kernel(*refs):
    for n, ref in enumerate(refs[:-1]):
        refs[-1][n] = ref[...]


def stack(values):
    return pl.pallas_call(
        stack_kernel,
        out_shape=jax.ShapeDtypeStruct((len(values),) + values[0].shape, BF),
        in_specs=[pl.BlockSpec(memory_space=pltpu.VMEM)] * len(values),
        out_specs=pl.BlockSpec(memory_space=pltpu.VMEM),
        compiler_params=params(8),
        cost_estimate=cost(0, 4 * len(values) * values[0].size),
    )(*values)


def join_kernel(one_ref, two_ref, out_ref, sems):
    copies = [pltpu.make_async_copy(ref, out_ref.at[n], sems.at[n]) for n, ref in enumerate((one_ref, two_ref))]
    for copy in copies:
        copy.start()
    for copy in copies:
        copy.wait()


def join(one, two):
    return pl.pallas_call(
        join_kernel,
        out_shape=jax.ShapeDtypeStruct((2,) + one.shape, BF),
        in_specs=in_hbm(2),
        out_specs=pl.BlockSpec(memory_space=pltpu.VMEM),
        scratch_shapes=[pltpu.SemaphoreType.DMA((2,))],
        compiler_params=params(8),
        cost_estimate=cost(0, 8 * one.size),
    )(*kept(one, two))


def halves_kernel(one_ref, three_ref, low_ref, high_ref):
    half = low_ref.shape[0]
    low_ref[...] = one_ref[:half]
    high_ref[...] = three_ref[half:]


def halves(one, three):
    half = jax.ShapeDtypeStruct((one.shape[0] // 2,) + one.shape[1:], BF)
    return pl.pallas_call(
        halves_kernel,
        out_shape=[half, half],
        in_specs=[pl.BlockSpec(memory_space=pltpu.VMEM)] * 2,
        out_specs=[pl.BlockSpec(memory_space=pltpu.VMEM)] * 2,
        compiler_params=params(8),
        cost_estimate=cost(0, 4 * one.size),
    )(one, three)


def gather_short(own):
    return [own, move_u(own, 1), move_u(own, 2), move_u(own, -1)]


def ring_kernel(own_ref, one_ref, low_ref, high_ref, three_ref, out_ref):
    out_ref[0] = own_ref[...]
    out_ref[1] = one_ref[...]
    out_ref[2, :1] = low_ref[...]
    out_ref[2, 1:] = high_ref[...]
    out_ref[3] = three_ref[...]


def gather_ring(own):
    own = own.reshape((2, own.shape[0] // 2) + own.shape[1:])
    one, three = move_u(own, 1), move_u(own, -1)
    low, high = halves(one, three)
    group = pl.pallas_call(
        ring_kernel,
        out_shape=jax.ShapeDtypeStruct((SIDE,) + own.shape, BF),
        in_specs=in_vmem(5),
        out_specs=pl.BlockSpec(memory_space=pltpu.VMEM),
        compiler_params=params(8),
        cost_estimate=cost(0, 16 * own.size),
    )(own, one, move_u(low, 1), move_u(high, -1), three)
    return group.reshape(SIDE, 2 * own.shape[1], own.shape[2])


def gather_long(group):
    return [move_v(group, 1), move_v(group, -1)]


def gather_last(side, *others):
    low, high = halves(*side)
    return [move_v(after(low, *others), 1), move_v(after(high, *others), -1)]


def params(mib):
    return pltpu.CompilerParams(vmem_limit_bytes=mib * MIB)


def in_vmem(count):
    return [pl.BlockSpec(memory_space=pltpu.VMEM)] * count


def cost(flops, bytes_accessed, transcendentals=0):
    return pl.CostEstimate(flops=flops // 1024, bytes_accessed=bytes_accessed // 1024, transcendentals=0)


DEPTH = 4


class Stream:
    def __init__(self, index_ref, count, query_ref, output_ref, scratch):
        self.index_ref, self.count = index_ref, count
        self.refs = (query_ref, output_ref)
        self.buffers, self.sems = scratch[:2], scratch[2:]
        for n in range(min(DEPTH - 1, count)):
            self.start(n)

    def copy(self, n, side):
        width = self.buffers[0].shape[1]
        at = pl.ds(pl.multiple_of(self.index_ref[n] * width, width), width)
        source = self.refs[0].at[at, :] if side == 0 else self.refs[1].at[:, at]
        slot = n % DEPTH
        return pltpu.make_async_copy(source, self.buffers[side].at[slot], self.sems[side].at[slot])

    def start(self, n):
        self.copy(n, 0).start()
        self.copy(n, 1).start()

    def blocks(self):
        for n in range(self.count):
            if n + DEPTH - 1 < self.count:
                self.start(n + DEPTH - 1)
            self.copy(n, 0).wait()
            self.copy(n, 1).wait()
            yield n, self.buffers[0].at[n % DEPTH], self.buffers[1].at[n % DEPTH]


def stream_scratch(width):
    return [
        pltpu.VMEM((DEPTH, width, width), BF),
        pltpu.VMEM((DEPTH, width, width), BF),
        pltpu.SemaphoreType.DMA((DEPTH,)),
        pltpu.SemaphoreType.DMA((DEPTH,)),
    ]


def in_hbm(count):
    return [pl.BlockSpec(memory_space=pltpu.HBM)] * count


def kept(*weights):
    return [pltpu.with_memory_space_constraint(weight, pltpu.HBM) for weight in weights]


def gathered_kernel(counts, has_start, index_ref, query_ref, output_ref, *refs):
    x_refs, refs = refs[: len(counts)], refs[len(counts) :]
    start_refs, refs = (refs[:2], refs[2:]) if has_start else (None, refs)
    (q_ref, d_ref), scratch = refs[:2], refs[2:]
    chunks = [x_ref.at[n] for count, x_ref in zip(counts, x_refs) for n in range(count)]
    q = start_refs[0][...] if has_start else None
    d = start_refs[1][...] if has_start else None
    for n, query_block, output_block in Stream(index_ref, len(chunks), query_ref, output_ref, scratch).blocks():
        term = dot(chunks[n][0], query_block[...], NN)
        q = term if q is None else q + term
        term = dot(chunks[n][1], output_block[...], NT)
        d = term if d is None else d + term
    q_ref[...] = q.astype(q_ref.dtype)
    d_ref[...] = d.astype(d_ref.dtype)


def gathered_dots(index, parts, query_weight, output_weight, start, out_type):
    rows, width = parts[0].shape[2:]
    cols = query_weight.shape[1]
    counts = [part.shape[0] for part in parts]
    count = sum(counts)
    return pl.pallas_call(
        functools.partial(gathered_kernel, counts, start is not None),
        out_shape=[jax.ShapeDtypeStruct((rows, cols), out_type)] * 2,
        in_specs=[pl.BlockSpec(memory_space=pltpu.SMEM)]
        + in_hbm(2)
        + in_vmem(len(parts) + (0 if start is None else 2)),
        out_specs=in_vmem(2),
        scratch_shapes=stream_scratch(width),
        compiler_params=params(8),
        cost_estimate=cost(4 * count * rows * width * cols, 4 * count * (rows + cols) * width),
    )(index, *kept(query_weight, output_weight), *parts, *([] if start is None else start))


def terms_kernel(count, index_ref, query_ref, output_ref, c_ref, d_ref, *refs):
    out_refs, scratch = refs[:-4], refs[-4:]
    targets = [(ref, at) for ref in out_refs for at in range(0, ref.shape[0], 2)]
    for n, query_block, output_block in Stream(index_ref, count, query_ref, output_ref, scratch).blocks():
        out_ref, at = targets[n]
        out_ref[at] = dot(c_ref[...], output_block[...], NN).astype(BF)
        out_ref[at + 1] = dot(d_ref[...], query_block[...], NT).astype(BF)


def scatter_terms(context, d_queries, query_weight, output_weight):
    rows, inner = context.shape
    width = query_weight.shape[0] // ENC

    def call(place, out_tiles, *others):
        count = place.shape[0]
        return pl.pallas_call(
            functools.partial(terms_kernel, count),
            out_shape=[jax.ShapeDtypeStruct((tiles, rows, width), BF) for tiles in out_tiles],
            in_specs=[pl.BlockSpec(memory_space=pltpu.SMEM)] + in_hbm(2) + in_vmem(2),
            out_specs=in_vmem(len(out_tiles)),
            scratch_shapes=stream_scratch(width),
            compiler_params=params(8),
            cost_estimate=cost(4 * count * rows * inner * width, 4 * count * (2 * rows + inner) * width),
        )(place, *kept(query_weight, output_weight), after(context, *others), d_queries)

    return call


def plus(*values):
    return sum(value.astype(F32) for value in values).astype(BF)


def pass_on_kernel(g3_ref, g1_ref, low_ref, high_ref, far_low_ref, far_high_ref, up_ref, down_ref):
    for n in range(2):
        up_ref[n] = plus(g3_ref[n], low_ref[n])
        up_ref[n + 2] = g3_ref[n + 2]
        down_ref[n] = g1_ref[n]
        down_ref[n + 2] = plus(g1_ref[n + 2], high_ref[n])
    for n in range(4):
        up_ref[n + 4] = far_low_ref[n]
        down_ref[n + 4] = far_high_ref[n]


def pass_on(g3, g1, low, high, far_low, far_high):
    return pl.pallas_call(
        pass_on_kernel,
        out_shape=[jax.ShapeDtypeStruct((8,) + g3.shape[1:], BF)] * 2,
        in_specs=in_vmem(6),
        out_specs=in_vmem(2),
        compiler_params=params(8),
        cost_estimate=cost(g3.size, 8 * g3.size),
    )(g3, g1, low, high, far_low, far_high)


def add_half_kernel(first, x_ref, part_ref, out_ref):
    for n in range(4):
        at, other = (n, n + 4) if first else (n + 4, n)
        out_ref[at] = plus(x_ref[at], part_ref[n + 4])
        out_ref[other] = x_ref[other]


def add_half(x, part, first):
    return pl.pallas_call(
        functools.partial(add_half_kernel, first),
        out_shape=jax.ShapeDtypeStruct(x.shape, BF),
        in_specs=in_vmem(2),
        out_specs=pl.BlockSpec(memory_space=pltpu.VMEM),
        compiler_params=params(8),
        cost_estimate=cost(x.size, 4 * x.size),
    )(x, part)


def add_pieces_kernel(*refs):
    r3_ref, r1_ref = refs[4:6]
    for n in range(4):
        tiles = refs[n].shape[0]
        for m in range(tiles):
            refs[6 + n][m] = plus(refs[n][m], r3_ref[n * tiles + m], r1_ref[n * tiles + m])


def add_pieces(pieces, r3, r1):
    return pl.pallas_call(
        add_pieces_kernel,
        out_shape=[jax.ShapeDtypeStruct(pieces[0].shape, BF)] * 4,
        in_specs=in_vmem(6),
        out_specs=in_vmem(4),
        compiler_params=params(8),
        cost_estimate=cost(8 * r3.size, 8 * r3.size),
    )(*pieces, r3, r1)


def move_pieces(pieces):
    return move_u(pieces[1], -1), move_u(pieces[2], 2), move_u(pieces[3], 1)


def finish_kernel(*refs):
    for n, ref in enumerate(refs[4:]):
        ref[...] = plus(*[part[n] for part in refs[:4]])


def finish(*parts):
    tiles = parts[0].shape[0]
    return pl.pallas_call(
        finish_kernel,
        out_shape=[jax.ShapeDtypeStruct(parts[0].shape[1:], BF)] * tiles,
        in_specs=in_vmem(4),
        out_specs=in_vmem(tiles),
        compiler_params=params(8),
        cost_estimate=cost(4 * parts[0].size, 10 * parts[0].size),
    )(*parts)


def project_kernel(pairs, key_ref, value_ref, *refs):
    x_refs, (k_ref, v_ref) = refs[:pairs], refs[pairs:]
    x = jnp.concatenate([ref[...].reshape(-1, ref.shape[-1]) for ref in x_refs], axis=0)
    k_ref[...] = dot(x, key_ref[...], NN).astype(BF)
    v_ref[...] = dot(x, value_ref[...], NN).astype(BF)


def project(pairs, key_weight, value_weight):
    features, cols = key_weight.shape
    rows = sum(pair.shape[0] * pair.shape[1] for pair in pairs)
    return pl.pallas_call(
        functools.partial(project_kernel, len(pairs)),
        out_shape=[jax.ShapeDtypeStruct((rows, cols), BF)] * 2,
        in_specs=in_vmem(2 + len(pairs)),
        out_specs=in_vmem(2),
        compiler_params=params(8),
        cost_estimate=cost(4 * rows * features * cols, 4 * (rows + cols) * features),
    )(key_weight, value_weight, *pairs)


def pair_kernel(groups, key_ref, value_ref, *refs):
    d_refs, out_refs = refs[: 2 * groups], refs[2 * groups :]
    tile = key_ref.shape[1]
    rows = d_refs[0].shape[0] // SIDE
    for n in range(key_ref.shape[0] // tile):
        targets = [(ref, m) for ref in out_refs for m in range(ref.shape[0])]
        for g in range(groups):
            total = dot(d_refs[2 * g][...], key_ref[n * tile : (n + 1) * tile, :], NT)
            total = (total + dot(d_refs[2 * g + 1][...], value_ref[n * tile : (n + 1) * tile, :], NT)).astype(BF)
            for m in range(SIDE):
                out_ref, at = targets[g * SIDE + m]
                out_ref[at, n * rows : (n + 1) * rows, :] = total[m * rows : (m + 1) * rows]


def pair_dots(grads, key_weight, value_weight, outs):
    rows, inner = grads[0].shape
    features = key_weight.shape[0]
    shape = (rows // SIDE * (features // inner), inner)
    groups = len(grads) // 2
    return pl.pallas_call(
        functools.partial(pair_kernel, groups),
        out_shape=[jax.ShapeDtypeStruct((chunks,) + shape, BF) for chunks in outs],
        in_specs=in_vmem(2 + len(grads)),
        out_specs=in_vmem(len(outs)),
        compiler_params=params(8),
        cost_estimate=cost(4 * groups * rows * inner * features, 4 * (groups * rows + inner) * features),
    )(key_weight, value_weight, *grads)


def attention_kernel(chunks, q_ref, d_ref, *refs):
    parts = len(chunks)
    keys, values = refs[:parts], refs[parts : 2 * parts]
    context_ref, dq_ref = refs[2 * parts : 2 * parts + 2]
    dk_refs, dv_refs = refs[2 * parts + 2 : 2 * parts + 6], refs[2 * parts + 6 :]
    scale = HEAD ** (-0.5)
    spans = q_ref.shape[0] // SPAN
    own = 256 // ENC
    places = [(part, n * spans * own) for part, count in enumerate(chunks) for n in range(count)]

    def span_rows(refs, c, cols):
        return jnp.concatenate([refs[part][at + c * own : at + (c + 1) * own, cols] for part, at in places], axis=0)

    for c in range(spans):
        rows = slice(c * SPAN, (c + 1) * SPAN)
        heads = [slice(h * HEAD, (h + 1) * HEAD) for h in range(q_ref.shape[1] // HEAD)]
        q, d = [q_ref[rows, cols] for cols in heads], [d_ref[rows, cols] for cols in heads]
        k, v = [span_rows(keys, c, cols) for cols in heads], [span_rows(values, c, cols) for cols in heads]
        scores = [dot(a, b, NT) * scale for a, b in zip(q, k)]
        d_attention = [dot(a, b, NT) for a, b in zip(d, v)]
        exponent = [jnp.exp(a - jnp.max(a, axis=-1, keepdims=True)) for a in scores]
        attention = [a * (1.0 / jnp.sum(a, axis=-1, keepdims=True)) for a in exponent]
        low = [a.astype(BF) for a in attention]
        inner = [jnp.sum(a * b, axis=-1, keepdims=True) for a, b in zip(attention, d_attention)]
        d_scores = [
            (a * (b - c) * scale).astype(BF) for a, b, c in zip(attention, d_attention, inner)
        ]
        for h, cols in enumerate(heads):
            context_ref[rows, cols] = dot(low[h], v[h], NN).astype(BF)
            dq_ref[rows, cols] = dot(d_scores[h], k[h], NN).astype(BF)
        for h, cols in enumerate(heads):
            dk = dot(d_scores[h], q[h], TN).astype(BF)
            dv = dot(low[h], d[h], TN).astype(BF)
            for n in range(ENC):
                at = (n % SIDE) * spans * own + c * own
                dk_refs[n // SIDE][at : at + own, cols] = dk[n * own : (n + 1) * own]
                dv_refs[n // SIDE][at : at + own, cols] = dv[n * own : (n + 1) * own]


def attend(queries, d_context, keys, values):
    rows, cols = queries.shape
    group_rows = sum(k.shape[0] for k in keys) // SIDE
    chunks = [k.shape[0] * ENC // (SIDE * group_rows) for k in keys]
    row_out = jax.ShapeDtypeStruct((rows, cols), BF)
    group = jax.ShapeDtypeStruct((group_rows, cols), BF)
    out = pl.pallas_call(
        functools.partial(attention_kernel, chunks),
        out_shape=[row_out] * 2 + [group] * 8,
        in_specs=in_vmem(2 + 2 * len(keys)),
        out_specs=in_vmem(10),
        compiler_params=params(8),
        cost_estimate=cost(12 * rows * 256 * cols, 20 * 1024 * cols, rows * 1024),
    )(queries, d_context, *keys, *values)
    return out[0], out[1], out[2:6], out[6:]


def on_device(
    hidden,
    query_weight,
    key_weight,
    value_weight,
    output_weight,
    neighbour_states,
    neighbour_slot,
    d_output,
):
    index = relative_index()
    features, cols = key_weight.shape
    local = neighbour_states.shape[2]
    chunk = neighbour_states.shape[1] // ENC
    used = neighbour_slot.size
    slot_shard = neighbour_slot.reshape(-1) // SEQ

    near = gather_short(join(hidden, d_output))
    arrived = lax.all_to_all(
        neighbour_states.reshape(SEQ * ENC, chunk, local), AXES, split_axis=0, concat_axis=0, tiled=True
    )
    near = stack([after(near[0], arrived)] + near[1:])
    side = gather_long(near)
    arrived = arrived.reshape(SEQ, ENC, chunk, local)
    picked = jnp.take(arrived, slot_shard, axis=1)
    picked = picked.transpose(1, 2, 0, 3).reshape(used * chunk, features)
    state_near = gather_ring(picked)
    state_side = gather_long(state_near)

    q_d = gathered_dots(index[0], [near], query_weight, output_weight, None, F32)
    kv_near = project([state_near], key_weight, value_weight)
    far = gather_last(side, *q_d)
    q_d = gathered_dots(
        jnp.concatenate([index[1], index[3]]), side, query_weight, output_weight, q_d, F32
    )
    state_far = gather_last(state_side, *q_d, *kv_near)
    kv_side = project(state_side, key_weight, value_weight)
    queries, d_context = gathered_dots(index[2], far, query_weight, output_weight, q_d, BF)
    state_far[0] = after(state_far[0], queries, *kv_side)
    kv_far = project(state_far, key_weight, value_weight)
    keys, values = zip(kv_near, kv_side, kv_far)

    context, d_queries, d_keys, d_values = attend(queries, d_context, keys, values)
    grads = {k: [d_keys[n], d_values[n]] for n, k in enumerate((0, 1, 3, 2))}

    both_terms = scatter_terms(context, d_queries, query_weight, output_weight)
    far = pair_dots(grads[2], key_weight, value_weight, [2, 2])
    from_low, from_high = move_v(far[0], 1), move_v(far[1], -1)
    both_far = both_terms(index[2], [4, 4], far[0])
    grads[3][0] = after(grads[3][0], *both_far)
    rest = pair_dots(grads[3] + grads[1] + grads[0], key_weight, value_weight, [4, 4, 1, 1, 1, 1])
    up, down = pass_on(rest[0], rest[1], from_low, from_high, *both_far)
    from_up, from_down = move_v(up, 1), move_v(down, -1)
    both_side = both_terms(jnp.concatenate([index[3], index[1]]), [8, 8], up)
    pieces = add_pieces(rest[2:], from_up, from_down)
    g3 = add_half(both_side[0], after(from_up, *pieces), True)
    g1 = add_half(both_side[1], after(from_down, g3), False)
    r3, r1 = move_v(g3, 1), move_v(g1, -1)
    (summed,) = finish(pieces[0], *move_pieces(pieces))
    both_near = both_terms(index[0], [2] * 4, g3, summed)
    both_pieces = add_pieces(both_near, after(r3, summed), r1)
    output, d_hidden = finish(both_pieces[0], *move_pieces(both_pieces))

    placing = lax.broadcasted_iota(jnp.int32, (ENC, used), 0) == slot_shard[None, :]
    spread = summed.reshape(-1, used, chunk, cols // local, local).transpose(0, 3, 1, 2, 4)
    spread = spread.reshape(SEQ, used, chunk, local)
    rank = jnp.argmax(placing, axis=1)
    spread = jnp.take(spread, rank, axis=1)
    spread = jnp.where(jnp.any(placing, axis=1)[None, :, None, None], spread, 0)
    back = lax.all_to_all(
        after(spread, *both_pieces).reshape(SEQ * ENC, chunk, local), AXES, split_axis=0, concat_axis=0, tiled=True
    )
    d_states = back.reshape(neighbour_states.shape)
    return (output, d_hidden, d_states)


def solution(mesh):
    in_specs = (
        P("seq", "enc"),
        P(None, "enc"),
        P(None, "enc"),
        P(None, "enc"),
        P("enc", None),
        P("enc", None, "seq"),
        P("seq", None),
        P("seq", "enc"),
    )
    out_specs = (P("seq", "enc"), P("seq", "enc"), P("enc", None, "seq"))
    return jax.shard_map(
        on_device, mesh=mesh, in_specs=in_specs, out_specs=out_specs, check_vma=False
    )
```

```python
import functools

import jax
import jax.numpy as jnp
from jax import lax
from jax.experimental import pallas as pl
from jax.experimental.pallas import tpu as pltpu
from jax.sharding import PartitionSpec as P

HEAD = 128
SPAN = 64
SEQ = 8
SIDE = 4
ENC = SIDE * SIDE
BF = jnp.bfloat16
F32 = jnp.float32
AXES = ("seq", "enc")
MIB = 1024 * 1024
NT = (((1,), (1,)), ((), ()))
NN = (((1,), (0,)), ((), ()))
TN = (((0,), (0,)), ((), ()))


def dot(a, b, dims):
    return lax.dot_general(a, b, dims, preferred_element_type=F32)


def shift_table(long_phase, shift):
    pairs = []
    for seq in range(SEQ):
        for z in range(SIDE):
            for x in range(SIDE):
                if (seq % 2 == 0) == long_phase:
                    to_z, to_x = (z + shift) % SIDE, x
                else:
                    to_z, to_x = z, (x + shift) % SIDE
                pairs.append((seq * ENC + z * SIDE + x, seq * ENC + to_z * SIDE + to_x))
    return pairs


def move_u(value, shift):
    return lax.ppermute(value, AXES, shift_table(False, shift))


def move_v(value, shift):
    return lax.ppermute(value, AXES, shift_table(True, shift))


def relative_index():
    seq, enc = lax.axis_index("seq"), lax.axis_index("enc")
    z, x = enc // SIDE, enc % SIDE
    even = seq % 2 == 0
    u, v = jnp.where(even, x, z), jnp.where(even, z, x)
    k = lax.broadcasted_iota(jnp.int32, (SIDE, SIDE), 0)
    j = lax.broadcasted_iota(jnp.int32, (SIDE, SIDE), 1)
    uu, vv = (u - j) % SIDE, (v - k) % SIDE
    return jnp.where(even, vv * SIDE + uu, uu * SIDE + vv).astype(jnp.int32)


def after(value, *others):
    return lax.optimization_barrier((value, *others))[0]


def stack_kernel(*refs):
    for n, ref in enumerate(refs[:-1]):
        refs[-1][n] = ref[...]


def stack(values):
    return pl.pallas_call(
        stack_kernel,
        out_shape=jax.ShapeDtypeStruct((len(values),) + values[0].shape, BF),
        in_specs=[pl.BlockSpec(memory_space=pltpu.VMEM)] * len(values),
        out_specs=pl.BlockSpec(memory_space=pltpu.VMEM),
        compiler_params=params(8),
        cost_estimate=cost(0, 4 * len(values) * values[0].size),
    )(*values)


def join_kernel(one_ref, two_ref, out_ref, sems):
    copies = [pltpu.make_async_copy(ref, out_ref.at[n], sems.at[n]) for n, ref in enumerate((one_ref, two_ref))]
    for copy in copies:
        copy.start()
    for copy in copies:
        copy.wait()


def join(one, two):
    return pl.pallas_call(
        join_kernel,
        out_shape=jax.ShapeDtypeStruct((2,) + one.shape, BF),
        in_specs=in_hbm(2),
        out_specs=pl.BlockSpec(memory_space=pltpu.VMEM),
        scratch_shapes=[pltpu.SemaphoreType.DMA((2,))],
        compiler_params=params(8),
        cost_estimate=cost(0, 8 * one.size),
    )(*kept(one, two))


def halves_kernel(one_ref, three_ref, low_ref, high_ref):
    half = low_ref.shape[0]
    low_ref[...] = one_ref[:half]
    high_ref[...] = three_ref[half:]


def halves(one, three):
    half = jax.ShapeDtypeStruct((one.shape[0] // 2,) + one.shape[1:], BF)
    return pl.pallas_call(
        halves_kernel,
        out_shape=[half, half],
        in_specs=[pl.BlockSpec(memory_space=pltpu.VMEM)] * 2,
        out_specs=[pl.BlockSpec(memory_space=pltpu.VMEM)] * 2,
        compiler_params=params(8),
        cost_estimate=cost(0, 4 * one.size),
    )(one, three)


def gather_short(own):
    return [own, move_u(own, 1), move_u(own, 2), move_u(own, -1)]


def ring_kernel(own_ref, one_ref, low_ref, high_ref, three_ref, out_ref):
    out_ref[0] = own_ref[...]
    out_ref[1] = one_ref[...]
    out_ref[2, :1] = low_ref[...]
    out_ref[2, 1:] = high_ref[...]
    out_ref[3] = three_ref[...]


def gather_ring(own):
    own = own.reshape((2, own.shape[0] // 2) + own.shape[1:])
    one, three = move_u(own, 1), move_u(own, -1)
    low, high = halves(one, three)
    group = pl.pallas_call(
        ring_kernel,
        out_shape=jax.ShapeDtypeStruct((SIDE,) + own.shape, BF),
        in_specs=in_vmem(5),
        out_specs=pl.BlockSpec(memory_space=pltpu.VMEM),
        compiler_params=params(8),
        cost_estimate=cost(0, 16 * own.size),
    )(own, one, move_u(low, 1), move_u(high, -1), three)
    return group.reshape(SIDE, 2 * own.shape[1], own.shape[2])


def gather_long(group):
    return [move_v(group, 1), move_v(group, -1)]


def gather_last(side, *others):
    low, high = halves(*side)
    return [move_v(after(low, *others), 1), move_v(after(high, *others), -1)]


def params(mib):
    return pltpu.CompilerParams(vmem_limit_bytes=mib * MIB)


def in_vmem(count):
    return [pl.BlockSpec(memory_space=pltpu.VMEM)] * count


def cost(flops, bytes_accessed, transcendentals=0):
    return pl.CostEstimate(flops=flops // 1024, bytes_accessed=bytes_accessed // 1024, transcendentals=0)


DEPTH = 4


class Stream:
    def __init__(self, index_ref, count, query_ref, output_ref, scratch):
        self.index_ref, self.count = index_ref, count
        self.refs = (query_ref, output_ref)
        self.buffers, self.sems = scratch[:2], scratch[2:]
        for n in range(min(DEPTH - 1, count)):
            self.start(n)

    def copy(self, n, side):
        width = self.buffers[0].shape[1]
        at = pl.ds(pl.multiple_of(self.index_ref[n] * width, width), width)
        source = self.refs[0].at[at, :] if side == 0 else self.refs[1].at[:, at]
        slot = n % DEPTH
        return pltpu.make_async_copy(source, self.buffers[side].at[slot], self.sems[side].at[slot])

    def start(self, n):
        self.copy(n, 0).start()
        self.copy(n, 1).start()

    def blocks(self):
        for n in range(self.count):
            if n + DEPTH - 1 < self.count:
                self.start(n + DEPTH - 1)
            self.copy(n, 0).wait()
            self.copy(n, 1).wait()
            yield n, self.buffers[0].at[n % DEPTH], self.buffers[1].at[n % DEPTH]


def stream_scratch(width):
    return [
        pltpu.VMEM((DEPTH, width, width), BF),
        pltpu.VMEM((DEPTH, width, width), BF),
        pltpu.SemaphoreType.DMA((DEPTH,)),
        pltpu.SemaphoreType.DMA((DEPTH,)),
    ]


def in_hbm(count):
    return [pl.BlockSpec(memory_space=pltpu.HBM)] * count


def kept(*weights):
    return [pltpu.with_memory_space_constraint(weight, pltpu.HBM) for weight in weights]


def gathered_kernel(counts, has_start, index_ref, query_ref, output_ref, *refs):
    x_refs, refs = refs[: len(counts)], refs[len(counts) :]
    start_refs, refs = (refs[:2], refs[2:]) if has_start else (None, refs)
    (q_ref, d_ref), scratch = refs[:2], refs[2:]
    chunks = [x_ref.at[n] for count, x_ref in zip(counts, x_refs) for n in range(count)]
    q = start_refs[0][...] if has_start else None
    d = start_refs[1][...] if has_start else None
    for n, query_block, output_block in Stream(index_ref, len(chunks), query_ref, output_ref, scratch).blocks():
        term = dot(chunks[n][0], query_block[...], NN)
        q = term if q is None else q + term
        term = dot(chunks[n][1], output_block[...], NT)
        d = term if d is None else d + term
    q_ref[...] = q.astype(q_ref.dtype)
    d_ref[...] = d.astype(d_ref.dtype)


def gathered_dots(index, parts, query_weight, output_weight, start, out_type):
    rows, width = parts[0].shape[2:]
    cols = query_weight.shape[1]
    counts = [part.shape[0] for part in parts]
    count = sum(counts)
    return pl.pallas_call(
        functools.partial(gathered_kernel, counts, start is not None),
        out_shape=[jax.ShapeDtypeStruct((rows, cols), out_type)] * 2,
        in_specs=[pl.BlockSpec(memory_space=pltpu.SMEM)]
        + in_hbm(2)
        + in_vmem(len(parts) + (0 if start is None else 2)),
        out_specs=in_vmem(2),
        scratch_shapes=stream_scratch(width),
        compiler_params=params(8),
        cost_estimate=cost(4 * count * rows * width * cols, 4 * count * (rows + cols) * width),
    )(index, *kept(query_weight, output_weight), *parts, *([] if start is None else start))


def terms_kernel(count, index_ref, query_ref, output_ref, c_ref, d_ref, *refs):
    out_refs, scratch = refs[:-4], refs[-4:]
    targets = [(ref, at) for ref in out_refs for at in range(0, ref.shape[0], 2)]
    for n, query_block, output_block in Stream(index_ref, count, query_ref, output_ref, scratch).blocks():
        out_ref, at = targets[n]
        out_ref[at] = dot(c_ref[...], output_block[...], NN).astype(BF)
        out_ref[at + 1] = dot(d_ref[...], query_block[...], NT).astype(BF)


def scatter_terms(context, d_queries, query_weight, output_weight):
    rows, inner = context.shape
    width = query_weight.shape[0] // ENC

    def call(place, out_tiles, *others):
        count = place.shape[0]
        return pl.pallas_call(
            functools.partial(terms_kernel, count),
            out_shape=[jax.ShapeDtypeStruct((tiles, rows, width), BF) for tiles in out_tiles],
            in_specs=[pl.BlockSpec(memory_space=pltpu.SMEM)] + in_hbm(2) + in_vmem(2),
            out_specs=in_vmem(len(out_tiles)),
            scratch_shapes=stream_scratch(width),
            compiler_params=params(8),
            cost_estimate=cost(4 * count * rows * inner * width, 4 * count * (2 * rows + inner) * width),
        )(place, *kept(query_weight, output_weight), after(context, *others), d_queries)

    return call


def plus(*values):
    return sum(value.astype(F32) for value in values).astype(BF)


def pass_on_kernel(g3_ref, g1_ref, low_ref, high_ref, far_low_ref, far_high_ref, up_ref, down_ref):
    for n in range(2):
        up_ref[n] = plus(g3_ref[n], low_ref[n])
        up_ref[n + 2] = g3_ref[n + 2]
        down_ref[n] = g1_ref[n]
        down_ref[n + 2] = plus(g1_ref[n + 2], high_ref[n])
    for n in range(4):
        up_ref[n + 4] = far_low_ref[n]
        down_ref[n + 4] = far_high_ref[n]


def pass_on(g3, g1, low, high, far_low, far_high):
    return pl.pallas_call(
        pass_on_kernel,
        out_shape=[jax.ShapeDtypeStruct((8,) + g3.shape[1:], BF)] * 2,
        in_specs=in_vmem(6),
        out_specs=in_vmem(2),
        compiler_params=params(8),
        cost_estimate=cost(g3.size, 8 * g3.size),
    )(g3, g1, low, high, far_low, far_high)


def add_half_kernel(first, x_ref, part_ref, out_ref):
    for n in range(4):
        at, other = (n, n + 4) if first else (n + 4, n)
        out_ref[at] = plus(x_ref[at], part_ref[n + 4])
        out_ref[other] = x_ref[other]


def add_half(x, part, first):
    return pl.pallas_call(
        functools.partial(add_half_kernel, first),
        out_shape=jax.ShapeDtypeStruct(x.shape, BF),
        in_specs=in_vmem(2),
        out_specs=pl.BlockSpec(memory_space=pltpu.VMEM),
        compiler_params=params(8),
        cost_estimate=cost(x.size, 4 * x.size),
    )(x, part)


def add_pieces_kernel(*refs):
    r3_ref, r1_ref = refs[4:6]
    for n in range(4):
        tiles = refs[n].shape[0]
        for m in range(tiles):
            refs[6 + n][m] = plus(refs[n][m], r3_ref[n * tiles + m], r1_ref[n * tiles + m])


def add_pieces(pieces, r3, r1):
    return pl.pallas_call(
        add_pieces_kernel,
        out_shape=[jax.ShapeDtypeStruct(pieces[0].shape, BF)] * 4,
        in_specs=in_vmem(6),
        out_specs=in_vmem(4),
        compiler_params=params(8),
        cost_estimate=cost(8 * r3.size, 8 * r3.size),
    )(*pieces, r3, r1)


def move_pieces(pieces):
    return move_u(pieces[1], -1), move_u(pieces[2], 2), move_u(pieces[3], 1)


def finish_kernel(*refs):
    for n, ref in enumerate(refs[4:]):
        ref[...] = plus(*[part[n] for part in refs[:4]])


def finish(*parts):
    tiles = parts[0].shape[0]
    return pl.pallas_call(
        finish_kernel,
        out_shape=[jax.ShapeDtypeStruct(parts[0].shape[1:], BF)] * tiles,
        in_specs=in_vmem(4),
        out_specs=in_vmem(tiles),
        compiler_params=params(8),
        cost_estimate=cost(4 * parts[0].size, 10 * parts[0].size),
    )(*parts)


def project_kernel(pairs, key_ref, value_ref, *refs):
    x_refs, (k_ref, v_ref) = refs[:pairs], refs[pairs:]
    x = jnp.concatenate([ref[...].reshape(-1, ref.shape[-1]) for ref in x_refs], axis=0)
    k_ref[...] = dot(x, key_ref[...], NN).astype(BF)
    v_ref[...] = dot(x, value_ref[...], NN).astype(BF)


def project(pairs, key_weight, value_weight):
    features, cols = key_weight.shape
    rows = sum(pair.shape[0] * pair.shape[1] for pair in pairs)
    return pl.pallas_call(
        functools.partial(project_kernel, len(pairs)),
        out_shape=[jax.ShapeDtypeStruct((rows, cols), BF)] * 2,
        in_specs=in_vmem(2 + len(pairs)),
        out_specs=in_vmem(2),
        compiler_params=params(8),
        cost_estimate=cost(4 * rows * features * cols, 4 * (rows + cols) * features),
    )(key_weight, value_weight, *pairs)


def pair_kernel(groups, key_ref, value_ref, *refs):
    d_refs, out_refs = refs[: 2 * groups], refs[2 * groups :]
    tile = key_ref.shape[1]
    rows = d_refs[0].shape[0] // SIDE
    for n in range(key_ref.shape[0] // tile):
        targets = [(ref, m) for ref in out_refs for m in range(ref.shape[0])]
        for g in range(groups):
            total = dot(d_refs[2 * g][...], key_ref[n * tile : (n + 1) * tile, :], NT)
            total = (total + dot(d_refs[2 * g + 1][...], value_ref[n * tile : (n + 1) * tile, :], NT)).astype(BF)
            for m in range(SIDE):
                out_ref, at = targets[g * SIDE + m]
                out_ref[at, n * rows : (n + 1) * rows, :] = total[m * rows : (m + 1) * rows]


def pair_dots(grads, key_weight, value_weight, outs):
    rows, inner = grads[0].shape
    features = key_weight.shape[0]
    shape = (rows // SIDE * (features // inner), inner)
    groups = len(grads) // 2
    return pl.pallas_call(
        functools.partial(pair_kernel, groups),
        out_shape=[jax.ShapeDtypeStruct((chunks,) + shape, BF) for chunks in outs],
        in_specs=in_vmem(2 + len(grads)),
        out_specs=in_vmem(len(outs)),
        compiler_params=params(8),
        cost_estimate=cost(4 * groups * rows * inner * features, 4 * (groups * rows + inner) * features),
    )(key_weight, value_weight, *grads)


def attention_kernel(chunks, q_ref, d_ref, *refs):
    parts = len(chunks)
    keys, values = refs[:parts], refs[parts : 2 * parts]
    context_ref, dq_ref = refs[2 * parts : 2 * parts + 2]
    dk_refs, dv_refs = refs[2 * parts + 2 : 2 * parts + 6], refs[2 * parts + 6 :]
    scale = HEAD ** (-0.5)
    spans = q_ref.shape[0] // SPAN
    own = 256 // ENC
    places = [(part, n * spans * own) for part, count in enumerate(chunks) for n in range(count)]

    def span_rows(refs, c, cols):
        return jnp.concatenate([refs[part][at + c * own : at + (c + 1) * own, cols] for part, at in places], axis=0)

    for c in range(spans):
        rows = slice(c * SPAN, (c + 1) * SPAN)
        heads = [slice(h * HEAD, (h + 1) * HEAD) for h in range(q_ref.shape[1] // HEAD)]
        q, d = [q_ref[rows, cols] for cols in heads], [d_ref[rows, cols] for cols in heads]
        k, v = [span_rows(keys, c, cols) for cols in heads], [span_rows(values, c, cols) for cols in heads]
        scores = [dot(a, b, NT) * scale for a, b in zip(q, k)]
        d_attention = [dot(a, b, NT) for a, b in zip(d, v)]
        exponent = [jnp.exp(a - jnp.max(a, axis=-1, keepdims=True)) for a in scores]
        attention = [a * (1.0 / jnp.sum(a, axis=-1, keepdims=True)) for a in exponent]
        low = [a.astype(BF) for a in attention]
        inner = [jnp.sum(a * b, axis=-1, keepdims=True) for a, b in zip(attention, d_attention)]
        d_scores = [
            (a * (b - c) * scale).astype(BF) for a, b, c in zip(attention, d_attention, inner)
        ]
        for h, cols in enumerate(heads):
            context_ref[rows, cols] = dot(low[h], v[h], NN).astype(BF)
            dq_ref[rows, cols] = dot(d_scores[h], k[h], NN).astype(BF)
        for h, cols in enumerate(heads):
            dk = dot(d_scores[h], q[h], TN).astype(BF)
            dv = dot(low[h], d[h], TN).astype(BF)
            for n in range(ENC):
                at = (n % SIDE) * spans * own + c * own
                dk_refs[n // SIDE][at : at + own, cols] = dk[n * own : (n + 1) * own]
                dv_refs[n // SIDE][at : at + own, cols] = dv[n * own : (n + 1) * own]


def attend(queries, d_context, keys, values):
    rows, cols = queries.shape
    group_rows = sum(k.shape[0] for k in keys) // SIDE
    chunks = [k.shape[0] * ENC // (SIDE * group_rows) for k in keys]
    row_out = jax.ShapeDtypeStruct((rows, cols), BF)
    group = jax.ShapeDtypeStruct((group_rows, cols), BF)
    out = pl.pallas_call(
        functools.partial(attention_kernel, chunks),
        out_shape=[row_out] * 2 + [group] * 8,
        in_specs=in_vmem(2 + 2 * len(keys)),
        out_specs=in_vmem(10),
        compiler_params=params(8),
        cost_estimate=cost(12 * rows * 256 * cols, 20 * 1024 * cols, rows * 1024),
    )(queries, d_context, *keys, *values)
    return out[0], out[1], out[2:6], out[6:]


def on_device(
    hidden,
    query_weight,
    key_weight,
    value_weight,
    output_weight,
    neighbour_states,
    neighbour_slot,
    d_output,
):
    index = relative_index()
    features, cols = key_weight.shape
    local = neighbour_states.shape[2]
    chunk = neighbour_states.shape[1] // ENC
    used = neighbour_slot.size
    slot_shard = neighbour_slot.reshape(-1) // SEQ

    near = gather_short(join(hidden, d_output))
    arrived = lax.all_to_all(
        neighbour_states.reshape(SEQ * ENC, chunk, local), AXES, split_axis=0, concat_axis=0, tiled=True
    )
    near = after(stack(near), arrived)
    side = gather_long(near)
    arrived = arrived.reshape(SEQ, ENC, chunk, local)
    picked = jnp.take(arrived, slot_shard, axis=1)
    picked = picked.transpose(1, 2, 0, 3).reshape(used * chunk, features)
    state_near = gather_ring(picked)
    state_side = gather_long(state_near)

    q_d = gathered_dots(index[0], [near], query_weight, output_weight, None, F32)
    kv_near = project([state_near], key_weight, value_weight)
    far = gather_last(side, *q_d)
    q_d = gathered_dots(
        jnp.concatenate([index[1], index[3]]), side, query_weight, output_weight, q_d, F32
    )
    state_far = gather_last(state_side, *q_d, *kv_near)
    kv_side = project(state_side, key_weight, value_weight)
    queries, d_context = gathered_dots(index[2], far, query_weight, output_weight, q_d, BF)
    state_far[0] = after(state_far[0], queries, *kv_side)
    kv_far = project(state_far, key_weight, value_weight)
    keys, values = zip(kv_near, kv_side, kv_far)

    context, d_queries, d_keys, d_values = attend(queries, d_context, keys, values)
    grads = {k: [d_keys[n], d_values[n]] for n, k in enumerate((0, 1, 3, 2))}

    both_terms = scatter_terms(context, d_queries, query_weight, output_weight)
    far = pair_dots(grads[2], key_weight, value_weight, [2, 2])
    from_low, from_high = move_v(far[0], 1), move_v(far[1], -1)
    both_far = both_terms(index[2], [4, 4], far[0])
    grads[3][0] = after(grads[3][0], *both_far)
    rest = pair_dots(grads[3] + grads[1] + grads[0], key_weight, value_weight, [4, 4, 1, 1, 1, 1])
    up, down = pass_on(rest[0], rest[1], from_low, from_high, *both_far)
    from_up, from_down = move_v(up, 1), move_v(down, -1)
    both_side = both_terms(jnp.concatenate([index[3], index[1]]), [8, 8], up)
    pieces = add_pieces(rest[2:], from_up, from_down)
    g3 = add_half(both_side[0], after(from_up, *pieces), True)
    g1 = add_half(both_side[1], after(from_down, g3), False)
    r3, r1 = move_v(g3, 1), move_v(g1, -1)
    (summed,) = finish(pieces[0], *move_pieces(pieces))
    both_near = both_terms(index[0], [2] * 4, g3, summed)
    both_pieces = add_pieces(both_near, after(r3, summed), r1)
    output, d_hidden = finish(both_pieces[0], *move_pieces(both_pieces))

    placing = lax.broadcasted_iota(jnp.int32, (ENC, used), 0) == slot_shard[None, :]
    spread = summed.reshape(-1, used, chunk, cols // local, local).transpose(0, 3, 1, 2, 4)
    spread = spread.reshape(SEQ, used, chunk, local)
    rank = jnp.argmax(placing, axis=1)
    spread = jnp.take(spread, rank, axis=1)
    spread = jnp.where(jnp.any(placing, axis=1)[None, :, None, None], spread, 0)
    back = lax.all_to_all(
        after(spread, *both_pieces).reshape(SEQ * ENC, chunk, local), AXES, split_axis=0, concat_axis=0, tiled=True
    )
    d_states = back.reshape(neighbour_states.shape)
    return (output, d_hidden, d_states)


def solution(mesh):
    in_specs = (
        P("seq", "enc"),
        P(None, "enc"),
        P(None, "enc"),
        P(None, "enc"),
        P("enc", None),
        P("enc", None, "seq"),
        P("seq", None),
        P("seq", "enc"),
    )
    out_specs = (P("seq", "enc"), P("seq", "enc"), P("enc", None, "seq"))
    return jax.shard_map(
        on_device, mesh=mesh, in_specs=in_specs, out_specs=out_specs, check_vma=False
    )
```

```python
import functools

import jax
import jax.numpy as jnp
from jax import lax
from jax.experimental import pallas as pl
from jax.experimental.pallas import tpu as pltpu
from jax.sharding import PartitionSpec as P

HEAD = 128
SPAN = 64
SEQ = 8
SIDE = 4
ENC = SIDE * SIDE
BF = jnp.bfloat16
F32 = jnp.float32
AXES = ("seq", "enc")
MIB = 1024 * 1024
NT = (((1,), (1,)), ((), ()))
NN = (((1,), (0,)), ((), ()))
TN = (((0,), (0,)), ((), ()))


def dot(a, b, dims):
    return lax.dot_general(a, b, dims, preferred_element_type=F32)


def shift_table(long_phase, shift):
    pairs = []
    for seq in range(SEQ):
        for z in range(SIDE):
            for x in range(SIDE):
                if (seq % 2 == 0) == long_phase:
                    to_z, to_x = (z + shift) % SIDE, x
                else:
                    to_z, to_x = z, (x + shift) % SIDE
                pairs.append((seq * ENC + z * SIDE + x, seq * ENC + to_z * SIDE + to_x))
    return pairs


def move_u(value, shift):
    return lax.ppermute(value, AXES, shift_table(False, shift))


def move_v(value, shift):
    return lax.ppermute(value, AXES, shift_table(True, shift))


def relative_index():
    seq, enc = lax.axis_index("seq"), lax.axis_index("enc")
    z, x = enc // SIDE, enc % SIDE
    even = seq % 2 == 0
    u, v = jnp.where(even, x, z), jnp.where(even, z, x)
    k = lax.broadcasted_iota(jnp.int32, (SIDE, SIDE), 0)
    j = lax.broadcasted_iota(jnp.int32, (SIDE, SIDE), 1)
    uu, vv = (u - j) % SIDE, (v - k) % SIDE
    return jnp.where(even, vv * SIDE + uu, uu * SIDE + vv).astype(jnp.int32)


def after(value, *others):
    return lax.optimization_barrier((value, *others))[0]


def stack_kernel(*refs):
    for n, ref in enumerate(refs[:-1]):
        refs[-1][n] = ref[...]


def stack(values):
    return pl.pallas_call(
        stack_kernel,
        out_shape=jax.ShapeDtypeStruct((len(values),) + values[0].shape, BF),
        in_specs=[pl.BlockSpec(memory_space=pltpu.VMEM)] * len(values),
        out_specs=pl.BlockSpec(memory_space=pltpu.VMEM),
        compiler_params=params(8),
        cost_estimate=cost(0, 4 * len(values) * values[0].size),
    )(*values)


def join_kernel(one_ref, two_ref, out_ref, sems):
    copies = [pltpu.make_async_copy(ref, out_ref.at[n], sems.at[n]) for n, ref in enumerate((one_ref, two_ref))]
    for copy in copies:
        copy.start()
    for copy in copies:
        copy.wait()


def join(one, two):
    return pl.pallas_call(
        join_kernel,
        out_shape=jax.ShapeDtypeStruct((2,) + one.shape, BF),
        in_specs=in_hbm(2),
        out_specs=pl.BlockSpec(memory_space=pltpu.VMEM),
        scratch_shapes=[pltpu.SemaphoreType.DMA((2,))],
        compiler_params=params(8),
        cost_estimate=cost(0, 8 * one.size),
    )(*kept(one, two))


def halves_kernel(one_ref, three_ref, low_ref, high_ref):
    half = low_ref.shape[0]
    low_ref[...] = one_ref[:half]
    high_ref[...] = three_ref[half:]


def halves(one, three):
    half = jax.ShapeDtypeStruct((one.shape[0] // 2,) + one.shape[1:], BF)
    return pl.pallas_call(
        halves_kernel,
        out_shape=[half, half],
        in_specs=[pl.BlockSpec(memory_space=pltpu.VMEM)] * 2,
        out_specs=[pl.BlockSpec(memory_space=pltpu.VMEM)] * 2,
        compiler_params=params(8),
        cost_estimate=cost(0, 4 * one.size),
    )(one, three)


def gather_short(own):
    return [own, move_u(own, 1), move_u(own, 2), move_u(own, -1)]


def ring_kernel(own_ref, one_ref, low_ref, high_ref, three_ref, out_ref):
    out_ref[0] = own_ref[...]
    out_ref[1] = one_ref[...]
    out_ref[2, :1] = low_ref[...]
    out_ref[2, 1:] = high_ref[...]
    out_ref[3] = three_ref[...]


def gather_ring(own):
    own = own.reshape((2, own.shape[0] // 2) + own.shape[1:])
    one, three = move_u(own, 1), move_u(own, -1)
    low, high = halves(one, three)
    group = pl.pallas_call(
        ring_kernel,
        out_shape=jax.ShapeDtypeStruct((SIDE,) + own.shape, BF),
        in_specs=in_vmem(5),
        out_specs=pl.BlockSpec(memory_space=pltpu.VMEM),
        compiler_params=params(8),
        cost_estimate=cost(0, 16 * own.size),
    )(own, one, move_u(low, 1), move_u(high, -1), three)
    return group.reshape(SIDE, 2 * own.shape[1], own.shape[2])


def gather_long(group):
    return [move_v(group, 1), move_v(group, -1)]


def gather_last(side, *others):
    low, high = halves(*side)
    return [move_v(after(low, *others), 1), move_v(after(high, *others), -1)]


def params(mib):
    return pltpu.CompilerParams(vmem_limit_bytes=mib * MIB)


def in_vmem(count):
    return [pl.BlockSpec(memory_space=pltpu.VMEM)] * count


def cost(flops, bytes_accessed, transcendentals=0):
    return pl.CostEstimate(flops=flops // 1024, bytes_accessed=bytes_accessed // 1024, transcendentals=0)


DEPTH = 4


class Stream:
    def __init__(self, index_ref, count, query_ref, output_ref, scratch):
        self.index_ref, self.count = index_ref, count
        self.refs = (query_ref, output_ref)
        self.buffers, self.sems = scratch[:2], scratch[2:]
        for n in range(min(DEPTH - 1, count)):
            self.start(n)

    def copy(self, n, side):
        width = self.buffers[0].shape[1]
        at = pl.ds(pl.multiple_of(self.index_ref[n] * width, width), width)
        source = self.refs[0].at[at, :] if side == 0 else self.refs[1].at[:, at]
        slot = n % DEPTH
        return pltpu.make_async_copy(source, self.buffers[side].at[slot], self.sems[side].at[slot])

    def start(self, n):
        self.copy(n, 0).start()
        self.copy(n, 1).start()

    def blocks(self):
        for n in range(self.count):
            if n + DEPTH - 1 < self.count:
                self.start(n + DEPTH - 1)
            self.copy(n, 0).wait()
            self.copy(n, 1).wait()
            yield n, self.buffers[0].at[n % DEPTH], self.buffers[1].at[n % DEPTH]


def stream_scratch(width):
    return [
        pltpu.VMEM((DEPTH, width, width), BF),
        pltpu.VMEM((DEPTH, width, width), BF),
        pltpu.SemaphoreType.DMA((DEPTH,)),
        pltpu.SemaphoreType.DMA((DEPTH,)),
    ]


def in_hbm(count):
    return [pl.BlockSpec(memory_space=pltpu.HBM)] * count


def kept(*weights):
    return [pltpu.with_memory_space_constraint(weight, pltpu.HBM) for weight in weights]


def gathered_kernel(counts, has_start, index_ref, query_ref, output_ref, *refs):
    x_refs, refs = refs[: len(counts)], refs[len(counts) :]
    start_refs, refs = (refs[:2], refs[2:]) if has_start else (None, refs)
    (q_ref, d_ref), scratch = refs[:2], refs[2:]
    chunks = [x_ref.at[n] for count, x_ref in zip(counts, x_refs) for n in range(count)]
    q = start_refs[0][...] if has_start else None
    d = start_refs[1][...] if has_start else None
    for n, query_block, output_block in Stream(index_ref, len(chunks), query_ref, output_ref, scratch).blocks():
        term = dot(chunks[n][0], query_block[...], NN)
        q = term if q is None else q + term
        term = dot(chunks[n][1], output_block[...], NT)
        d = term if d is None else d + term
    q_ref[...] = q.astype(q_ref.dtype)
    d_ref[...] = d.astype(d_ref.dtype)


def gathered_dots(index, parts, query_weight, output_weight, start, out_type):
    rows, width = parts[0].shape[2:]
    cols = query_weight.shape[1]
    counts = [part.shape[0] for part in parts]
    count = sum(counts)
    return pl.pallas_call(
        functools.partial(gathered_kernel, counts, start is not None),
        out_shape=[jax.ShapeDtypeStruct((rows, cols), out_type)] * 2,
        in_specs=[pl.BlockSpec(memory_space=pltpu.SMEM)]
        + in_hbm(2)
        + in_vmem(len(parts) + (0 if start is None else 2)),
        out_specs=in_vmem(2),
        scratch_shapes=stream_scratch(width),
        compiler_params=params(8),
        cost_estimate=cost(4 * count * rows * width * cols, 4 * count * (rows + cols) * width),
    )(index, *kept(query_weight, output_weight), *parts, *([] if start is None else start))


def terms_kernel(count, index_ref, query_ref, output_ref, c_ref, d_ref, *refs):
    out_refs, scratch = refs[:-4], refs[-4:]
    targets = [(ref, at) for ref in out_refs for at in range(0, ref.shape[0], 2)]
    for n, query_block, output_block in Stream(index_ref, count, query_ref, output_ref, scratch).blocks():
        out_ref, at = targets[n]
        out_ref[at] = dot(c_ref[...], output_block[...], NN).astype(BF)
        out_ref[at + 1] = dot(d_ref[...], query_block[...], NT).astype(BF)


def scatter_terms(context, d_queries, query_weight, output_weight):
    rows, inner = context.shape
    width = query_weight.shape[0] // ENC

    def call(place, out_tiles, *others):
        count = place.shape[0]
        return pl.pallas_call(
            functools.partial(terms_kernel, count),
            out_shape=[jax.ShapeDtypeStruct((tiles, rows, width), BF) for tiles in out_tiles],
            in_specs=[pl.BlockSpec(memory_space=pltpu.SMEM)] + in_hbm(2) + in_vmem(2),
            out_specs=in_vmem(len(out_tiles)),
            scratch_shapes=stream_scratch(width),
            compiler_params=params(8),
            cost_estimate=cost(4 * count * rows * inner * width, 4 * count * (2 * rows + inner) * width),
        )(place, *kept(query_weight, output_weight), after(context, *others), d_queries)

    return call


def plus(*values):
    return sum(value.astype(F32) for value in values).astype(BF)


def pass_on_kernel(g3_ref, g1_ref, low_ref, high_ref, far_low_ref, far_high_ref, up_ref, down_ref):
    for n in range(2):
        up_ref[n] = plus(g3_ref[n], low_ref[n])
        up_ref[n + 2] = g3_ref[n + 2]
        down_ref[n] = g1_ref[n]
        down_ref[n + 2] = plus(g1_ref[n + 2], high_ref[n])
    for n in range(4):
        up_ref[n + 4] = far_low_ref[n]
        down_ref[n + 4] = far_high_ref[n]


def pass_on(g3, g1, low, high, far_low, far_high):
    return pl.pallas_call(
        pass_on_kernel,
        out_shape=[jax.ShapeDtypeStruct((8,) + g3.shape[1:], BF)] * 2,
        in_specs=in_vmem(6),
        out_specs=in_vmem(2),
        compiler_params=params(8),
        cost_estimate=cost(g3.size, 8 * g3.size),
    )(g3, g1, low, high, far_low, far_high)


def add_half_kernel(first, x_ref, part_ref, out_ref):
    for n in range(4):
        at, other = (n, n + 4) if first else (n + 4, n)
        out_ref[at] = plus(x_ref[at], part_ref[n + 4])
        out_ref[other] = x_ref[other]


def add_half(x, part, first):
    return pl.pallas_call(
        functools.partial(add_half_kernel, first),
        out_shape=jax.ShapeDtypeStruct(x.shape, BF),
        in_specs=in_vmem(2),
        out_specs=pl.BlockSpec(memory_space=pltpu.VMEM),
        compiler_params=params(8),
        cost_estimate=cost(x.size, 4 * x.size),
    )(x, part)


def add_pieces_kernel(*refs):
    r3_ref, r1_ref = refs[3:5]
    for n in range(3):
        tiles = refs[n].shape[0]
        for m in range(tiles):
            at = (n + 1) * tiles + m
            refs[5 + n][m] = plus(refs[n][m], r3_ref[at], r1_ref[at])


def add_pieces(pieces, r3, r1):
    return pl.pallas_call(
        add_pieces_kernel,
        out_shape=[jax.ShapeDtypeStruct(pieces[0].shape, BF)] * 3,
        in_specs=in_vmem(5),
        out_specs=in_vmem(3),
        compiler_params=params(8),
        cost_estimate=cost(8 * r3.size, 8 * r3.size),
    )(*pieces[1:], r3, r1)


def move_pieces(pieces):
    return move_u(pieces[0], -1), move_u(pieces[1], 2), move_u(pieces[2], 1)


def finish_kernel(count, *refs):
    for n, ref in enumerate(refs[count:]):
        ref[...] = plus(*[part[n] for part in refs[:count]])


def finish(*parts):
    tiles = parts[0].shape[0]
    return pl.pallas_call(
        functools.partial(finish_kernel, len(parts)),
        out_shape=[jax.ShapeDtypeStruct(parts[0].shape[1:], BF)] * tiles,
        in_specs=in_vmem(len(parts)),
        out_specs=in_vmem(tiles),
        compiler_params=params(8),
        cost_estimate=cost(4 * parts[0].size, 10 * parts[0].size),
    )(*parts)


def project_kernel(pairs, key_ref, value_ref, *refs):
    x_refs, (k_ref, v_ref) = refs[:pairs], refs[pairs:]
    x = jnp.concatenate([ref[...].reshape(-1, ref.shape[-1]) for ref in x_refs], axis=0)
    k_ref[...] = dot(x, key_ref[...], NN).astype(BF)
    v_ref[...] = dot(x, value_ref[...], NN).astype(BF)


def project(pairs, key_weight, value_weight):
    features, cols = key_weight.shape
    rows = sum(pair.shape[0] * pair.shape[1] for pair in pairs)
    return pl.pallas_call(
        functools.partial(project_kernel, len(pairs)),
        out_shape=[jax.ShapeDtypeStruct((rows, cols), BF)] * 2,
        in_specs=in_vmem(2 + len(pairs)),
        out_specs=in_vmem(2),
        compiler_params=params(8),
        cost_estimate=cost(4 * rows * features * cols, 4 * (rows + cols) * features),
    )(key_weight, value_weight, *pairs)


def pair_kernel(groups, key_ref, value_ref, *refs):
    d_refs, out_refs = refs[: 2 * groups], refs[2 * groups :]
    tile = key_ref.shape[1]
    rows = d_refs[0].shape[0] // SIDE
    for n in range(key_ref.shape[0] // tile):
        targets = [(ref, m) for ref in out_refs for m in range(ref.shape[0])]
        for g in range(groups):
            total = dot(d_refs[2 * g][...], key_ref[n * tile : (n + 1) * tile, :], NT)
            total = (total + dot(d_refs[2 * g + 1][...], value_ref[n * tile : (n + 1) * tile, :], NT)).astype(BF)
            for m in range(SIDE):
                out_ref, at = targets[g * SIDE + m]
                out_ref[at, n * rows : (n + 1) * rows, :] = total[m * rows : (m + 1) * rows]


def pair_dots(grads, key_weight, value_weight, outs):
    rows, inner = grads[0].shape
    features = key_weight.shape[0]
    shape = (rows // SIDE * (features // inner), inner)
    groups = len(grads) // 2
    return pl.pallas_call(
        functools.partial(pair_kernel, groups),
        out_shape=[jax.ShapeDtypeStruct((chunks,) + shape, BF) for chunks in outs],
        in_specs=in_vmem(2 + len(grads)),
        out_specs=in_vmem(len(outs)),
        compiler_params=params(8),
        cost_estimate=cost(4 * groups * rows * inner * features, 4 * (groups * rows + inner) * features),
    )(key_weight, value_weight, *grads)


def attention_kernel(chunks, q_ref, d_ref, *refs):
    parts = len(chunks)
    keys, values = refs[:parts], refs[parts : 2 * parts]
    context_ref, dq_ref = refs[2 * parts : 2 * parts + 2]
    dk_refs, dv_refs = refs[2 * parts + 2 : 2 * parts + 6], refs[2 * parts + 6 :]
    scale = HEAD ** (-0.5)
    spans = q_ref.shape[0] // SPAN
    own = 256 // ENC
    places = [(part, n * spans * own) for part, count in enumerate(chunks) for n in range(count)]

    def span_rows(refs, c, cols):
        return jnp.concatenate([refs[part][at + c * own : at + (c + 1) * own, cols] for part, at in places], axis=0)

    for c in range(spans):
        rows = slice(c * SPAN, (c + 1) * SPAN)
        heads = [slice(h * HEAD, (h + 1) * HEAD) for h in range(q_ref.shape[1] // HEAD)]
        q, d = [q_ref[rows, cols] for cols in heads], [d_ref[rows, cols] for cols in heads]
        k, v = [span_rows(keys, c, cols) for cols in heads], [span_rows(values, c, cols) for cols in heads]
        scores = [dot(a, b, NT) * scale for a, b in zip(q, k)]
        d_attention = [dot(a, b, NT) for a, b in zip(d, v)]
        exponent = [jnp.exp(a - jnp.max(a, axis=-1, keepdims=True)) for a in scores]
        attention = [a * (1.0 / jnp.sum(a, axis=-1, keepdims=True)) for a in exponent]
        low = [a.astype(BF) for a in attention]
        inner = [jnp.sum(a * b, axis=-1, keepdims=True) for a, b in zip(attention, d_attention)]
        d_scores = [
            (a * (b - c) * scale).astype(BF) for a, b, c in zip(attention, d_attention, inner)
        ]
        for h, cols in enumerate(heads):
            context_ref[rows, cols] = dot(low[h], v[h], NN).astype(BF)
            dq_ref[rows, cols] = dot(d_scores[h], k[h], NN).astype(BF)
        for h, cols in enumerate(heads):
            dk = dot(d_scores[h], q[h], TN).astype(BF)
            dv = dot(low[h], d[h], TN).astype(BF)
            for n in range(ENC):
                at = (n % SIDE) * spans * own + c * own
                dk_refs[n // SIDE][at : at + own, cols] = dk[n * own : (n + 1) * own]
                dv_refs[n // SIDE][at : at + own, cols] = dv[n * own : (n + 1) * own]


def attend(queries, d_context, keys, values):
    rows, cols = queries.shape
    group_rows = sum(k.shape[0] for k in keys) // SIDE
    chunks = [k.shape[0] * ENC // (SIDE * group_rows) for k in keys]
    row_out = jax.ShapeDtypeStruct((rows, cols), BF)
    group = jax.ShapeDtypeStruct((group_rows, cols), BF)
    out = pl.pallas_call(
        functools.partial(attention_kernel, chunks),
        out_shape=[row_out] * 2 + [group] * 8,
        in_specs=in_vmem(2 + 2 * len(keys)),
        out_specs=in_vmem(10),
        compiler_params=params(8),
        cost_estimate=cost(12 * rows * 256 * cols, 20 * 1024 * cols, rows * 1024),
    )(queries, d_context, *keys, *values)
    return out[0], out[1], out[2:6], out[6:]


def on_device(
    hidden,
    query_weight,
    key_weight,
    value_weight,
    output_weight,
    neighbour_states,
    neighbour_slot,
    d_output,
):
    index = relative_index()
    features, cols = key_weight.shape
    local = neighbour_states.shape[2]
    chunk = neighbour_states.shape[1] // ENC
    used = neighbour_slot.size
    slot_shard = neighbour_slot.reshape(-1) // SEQ

    near = gather_short(join(hidden, d_output))
    arrived = lax.all_to_all(
        neighbour_states.reshape(SEQ * ENC, chunk, local), AXES, split_axis=0, concat_axis=0, tiled=True
    )
    near = after(stack(near), arrived)
    side = gather_long(near)
    arrived = arrived.reshape(SEQ, ENC, chunk, local)
    picked = jnp.take(arrived, slot_shard, axis=1)
    picked = picked.transpose(1, 2, 0, 3).reshape(used * chunk, features)
    state_near = gather_ring(picked)
    state_side = gather_long(state_near)

    q_d = gathered_dots(index[0], [near], query_weight, output_weight, None, F32)
    kv_near = project([state_near], key_weight, value_weight)
    far = gather_last(side, *q_d)
    q_d = gathered_dots(
        jnp.concatenate([index[1], index[3]]), side, query_weight, output_weight, q_d, F32
    )
    state_far = gather_last(state_side, *q_d, *kv_near)
    kv_side = project(state_side, key_weight, value_weight)
    queries, d_context = gathered_dots(index[2], far, query_weight, output_weight, q_d, BF)
    state_far[0] = after(state_far[0], queries, *kv_side)
    kv_far = project(state_far, key_weight, value_weight)
    keys, values = zip(kv_near, kv_side, kv_far)

    context, d_queries, d_keys, d_values = attend(queries, d_context, keys, values)
    grads = {k: [d_keys[n], d_values[n]] for n, k in enumerate((0, 1, 3, 2))}

    both_terms = scatter_terms(context, d_queries, query_weight, output_weight)
    far = pair_dots(grads[2], key_weight, value_weight, [2, 2])
    from_low, from_high = move_v(far[0], 1), move_v(far[1], -1)
    both_far = both_terms(index[2], [4, 4], far[0])
    grads[3][0] = after(grads[3][0], *both_far)
    rest = pair_dots(grads[3] + grads[1] + grads[0], key_weight, value_weight, [4, 4, 1, 1, 1, 1])
    up, down = pass_on(rest[0], rest[1], from_low, from_high, *both_far)
    from_up, from_down = move_v(up, 1), move_v(down, -1)
    both_side = both_terms(jnp.concatenate([index[3], index[1]]), [8, 8], up)
    pieces = add_pieces(rest[2:], from_up, from_down)
    g3 = add_half(both_side[0], after(from_up, *pieces), True)
    g1 = add_half(both_side[1], after(from_down, g3), False)
    r3, r1 = move_v(g3, 1), move_v(g1, -1)
    (summed,) = finish(rest[2], from_up, from_down, *move_pieces(pieces))
    both_near = both_terms(index[0], [2] * 4, g3, summed)
    both_pieces = add_pieces(both_near, after(r3, summed), r1)
    output, d_hidden = finish(both_near[0], r3, r1, *move_pieces(both_pieces))

    placing = lax.broadcasted_iota(jnp.int32, (ENC, used), 0) == slot_shard[None, :]
    spread = summed.reshape(-1, used, chunk, cols // local, local).transpose(0, 3, 1, 2, 4)
    spread = spread.reshape(SEQ, used, chunk, local)
    rank = jnp.argmax(placing, axis=1)
    spread = jnp.take(spread, rank, axis=1)
    spread = jnp.where(jnp.any(placing, axis=1)[None, :, None, None], spread, 0)
    back = lax.all_to_all(
        after(spread, *both_pieces).reshape(SEQ * ENC, chunk, local), AXES, split_axis=0, concat_axis=0, tiled=True
    )
    d_states = back.reshape(neighbour_states.shape)
    return (output, d_hidden, d_states)


def solution(mesh):
    in_specs = (
        P("seq", "enc"),
        P(None, "enc"),
        P(None, "enc"),
        P(None, "enc"),
        P("enc", None),
        P("enc", None, "seq"),
        P("seq", None),
        P("seq", "enc"),
    )
    out_specs = (P("seq", "enc"), P("seq", "enc"), P("enc", None, "seq"))
    return jax.shard_map(
        on_device, mesh=mesh, in_specs=in_specs, out_specs=out_specs, check_vma=False
    )
```
